32 devices in a mesh: gx: 8 (over z, y), gy: 4 (over x, core).
Axes of the slice: x: 2, y: 2, z: 4, core: 2. Of those that a mesh axis runs over, the one named last changes fastest.
Arguments:
- thermal_grid: float32 [32, 64, 128], P('gx', 'gy'), may hold values from -6 to 6
- average_blend_fraction: float32 [32, 64, 128], P('gx', 'gy'), may hold values from 0.05 to 0.95
- normalized_blend_variance: float32 [32, 64, 128], P('gx', 'gy'), may hold values from 0.002 to 0.5
- small_volume_mass: float32 [32, 64, 128], P('gx', 'gy'), may hold values from 0.01 to 0.1
- bare_scalar_decay: float32 [32, 64, 128], P('gx', 'gy'), may hold values from 0.05 to 1
- parent_block: int32 [32, 64, 128], P('gx', 'gy'), may hold values from 0 to 127, as said below
- species_given_block: float32 [128, 16, 128], P(('gx', 'gy')), may hold values from -6 to 6
- block_position: int32 [128], replicated, may hold values from 0 to 127, each once
- face_partners: int32 [128, 6], replicated, may hold values from 0 to 127, as said below
- reaction_increments: int32 [128], replicated, may hold values from 0 to 15, as said below
- chemical_coupling: float32 [16, 16], replicated, may hold values from -1.5 to 1.5
- species_thermal_weight: float32 [16], replicated, may hold values from -1.5 to 1.5
Outputs:
- species_next: float32 [128, 16, 128], P(('gx', 'gy'))
- temperature_next: float32 [32, 64, 128], P('gx', 'gy')
The draws below stay inside these ranges and needn't reach their ends.
Inputs may be any that keep to these rules, and one draw needn't show every extreme that they name: `parent_block`: each fine cell names the coarse cell under it after a shift of at most 2 fine cells along each dimension; every coarse cell is named. `face_partners`: A cell on the grid's border names itself in place of a missing neighbour; every coarse cell is named. `reaction_increments`: both ends are reached in every draw.
All inputs are finite; a program needn't handle non-finite values.
Results may differ from the reference program's by a relative error of at most 0.0003.
Values sent between devices are 32-bit elements; how exact they have to be, the bound alone decides.
A program may use at most 128 MiB of HBM per device.

```python
import math
import jax
import jax.numpy as jnp
from jax import lax

SMALL_ALONG_Z = 128
ETA = 128
SPEC = 16
SUBMAX = 16
STEPS = 2
JITTER = 2
CGZ = 8
CGX = 4
CGY = 4
BLOCK_COUNT = 128
SMALL_ALONG_X = 32
SMALL_ALONG_Y = 64


def numbering(key):
    return jax.random.permutation(jax.random.fold_in(key, 5), BLOCK_COUNT).astype(jnp.int32)


def parents(key):
    perm = numbering(key)
    shifts = jax.random.randint(jax.random.fold_in(key, 11), (3, SMALL_ALONG_X, SMALL_ALONG_Y, SMALL_ALONG_Z), -JITTER, JITTER + 1)
    xs = jnp.clip(jnp.arange(SMALL_ALONG_X)[:, None, None] + shifts[0], 0, SMALL_ALONG_X - 1)
    ys = jnp.clip(jnp.arange(SMALL_ALONG_Y)[None, :, None] + shifts[1], 0, SMALL_ALONG_Y - 1)
    zs = jnp.clip(jnp.arange(SMALL_ALONG_Z)[None, None, :] + shifts[2], 0, SMALL_ALONG_Z - 1)
    coarse = (xs // (SMALL_ALONG_X // CGX) * CGY + ys // (SMALL_ALONG_Y // CGY)) * CGZ + zs // (SMALL_ALONG_Z // CGZ)
    return perm[coarse].astype(jnp.int32)


def narrow_cells(key):
    owner = parents(key)
    picked = jax.random.permutation(jax.random.fold_in(key, 21), BLOCK_COUNT) < BLOCK_COUNT // 4
    sides = jax.random.randint(jax.random.fold_in(key, 22), (BLOCK_COUNT,), 0, 2)
    return (picked[owner], sides[owner])


def fresh_uniform(key, salt):
    return jax.random.uniform(jax.random.fold_in(key, salt), (SMALL_ALONG_X, SMALL_ALONG_Y, SMALL_ALONG_Z), jnp.float32)


def draw_parent_block(key, part):
    return parents(key)


def draw_average_blend_fraction(key, part):
    picked, sides = narrow_cells(key)
    base = fresh_uniform(key, 31)
    spread = 0.05 + 0.9 * base
    ends = 0.05 + 0.9 * sides.astype(jnp.float32)
    return jnp.clip(jnp.where(picked, ends, spread), 0.05, 0.95).astype(jnp.float32)


def draw_normalized_blend_variance(key, part):
    picked, sides = narrow_cells(key)
    base = fresh_uniform(key, 32)
    spread = jnp.exp(jnp.log(0.002) + base * (jnp.log(0.5) - jnp.log(0.002)))
    return jnp.clip(jnp.where(picked, 0.002, spread), 0.002, 0.5).astype(jnp.float32)


def draw_bare_scalar_decay(key, part):
    picked, sides = narrow_cells(key)
    base = fresh_uniform(key, 33)
    spread = jnp.exp(jnp.log(0.05) + base * (0.0 - jnp.log(0.05)))
    return jnp.clip(jnp.where(picked, 1.0, spread), 0.05, 1.0).astype(jnp.float32)


def draw_face_partners(key, part):
    perm = numbering(key)
    geo = jnp.arange(BLOCK_COUNT)
    cxs = geo // (CGY * CGZ)
    cys = geo // CGZ % CGY
    czs = geo % CGZ
    columns = []
    for axis_pick, offset in ((0, 1), (0, -1), (1, 1), (1, -1), (2, 1), (2, -1)):
        nx_cell = jnp.clip(cxs + offset, 0, CGX - 1) if axis_pick == 0 else cxs
        ny_cell = jnp.clip(cys + offset, 0, CGY - 1) if axis_pick == 1 else cys
        nz_cell = jnp.clip(czs + offset, 0, CGZ - 1) if axis_pick == 2 else czs
        columns.append((nx_cell * CGY + ny_cell) * CGZ + nz_cell)
    near_geo = jnp.stack(columns, axis=1)
    result = jnp.zeros((BLOCK_COUNT, 6), jnp.int32).at[perm].set(perm[near_geo])
    return result.astype(jnp.int32)


def draw_reaction_increments(key, part):
    first = jax.random.randint(jax.random.fold_in(key, 3), (BLOCK_COUNT,), 0, SUBMAX)
    second = jax.random.randint(jax.random.fold_in(key, 4), (BLOCK_COUNT,), 0, SUBMAX)
    values = first * second // (SUBMAX - 1)
    spots = jax.random.randint(jax.random.fold_in(key, 6), (2,), 0, BLOCK_COUNT // 2)
    values = values.at[spots[0]].set(SUBMAX - 1)
    values = values.at[BLOCK_COUNT // 2 + spots[1]].set(0)
    return values.astype(jnp.int32)


def block_levels(own_key, extent, cuts, low, largest):
    gain = 1.0
    for axis_at, blocks in cuts:
        steps = jax.random.uniform(jax.random.fold_in(jax.random.fold_in(own_key, 6), axis_at), (blocks,), jnp.float32, low / len(cuts), largest / len(cuts))
        gain = gain * jnp.repeat(jnp.exp(steps), extent[axis_at] // blocks).reshape((-1,) + (1,) * (len(extent) - 1 - axis_at))
    return gain


def normal_values(rng, extent, scale, reach, pieces=(), kind=jnp.bfloat16):
    values = jax.random.normal(rng, extent, jnp.float32) * scale
    if len(pieces) > 0:
        values = block_levels(rng, extent, pieces, -0.22, 0.18) * values
    return jnp.clip(values, min=-reach, max=reach).astype(kind)


def setup_inputs(seed: int = 0) -> dict:
    seeds = jax.random.split(jax.random.key(seed), 13)
    thermal_grid = normal_values(seeds[0], (SMALL_ALONG_X, SMALL_ALONG_Y, SMALL_ALONG_Z), 1.0, 6.0, ((0, 8), (1, 4)), jnp.float32)
    average_blend_fraction = draw_average_blend_fraction(jax.random.fold_in(seeds[12], 71), 0)
    normalized_blend_variance = draw_normalized_blend_variance(jax.random.fold_in(seeds[12], 71), 0)
    small_volume_mass = jnp.clip(jnp.exp(math.log(0.1) - 2.3025851 * jax.random.uniform(seeds[3], (SMALL_ALONG_X, SMALL_ALONG_Y, SMALL_ALONG_Z), jnp.float32) ** block_levels(seeds[3], (SMALL_ALONG_X, SMALL_ALONG_Y, SMALL_ALONG_Z), ((0, 8), (1, 4)), -0.2, 0.2)), 0.01, 0.1)
    bare_scalar_decay = draw_bare_scalar_decay(jax.random.fold_in(seeds[12], 71), 0)
    parent_block = draw_parent_block(jax.random.fold_in(seeds[12], 71), 0)
    species_given_block = normal_values(seeds[6], (BLOCK_COUNT, SPEC, ETA), 1.0, 6.0, ((0, 32),), jnp.float32)
    block_position = jax.random.permutation(seeds[7], BLOCK_COUNT).astype(jnp.int32)
    face_partners = draw_face_partners(jax.random.fold_in(seeds[12], 71), 0)
    reaction_increments = draw_reaction_increments(jax.random.fold_in(seeds[12], 71), 0)
    chemical_coupling = normal_values(seeds[10], (SPEC, SPEC), SPEC ** -0.5, 1.5, (), jnp.float32)
    species_thermal_weight = normal_values(seeds[11], (SPEC,), SPEC ** -0.5, 1.5, (), jnp.float32)
    return {"thermal_grid": thermal_grid, "average_blend_fraction": average_blend_fraction, "normalized_blend_variance": normalized_blend_variance, "small_volume_mass": small_volume_mass, "bare_scalar_decay": bare_scalar_decay, "parent_block": parent_block, "species_given_block": species_given_block, "block_position": block_position, "face_partners": face_partners, "reaction_increments": reaction_increments, "chemical_coupling": chemical_coupling, "species_thermal_weight": species_thermal_weight}


coupling = 0.05
mixing_rate = 0.2
react_rate = 0.5
prior_weight = 1.0
prior_flux = 0.5
thermal_diffusion = 0.1
damping_contribution = 0.3


def beta_table(average_blend_fraction, normalized_blend_variance):
    points = (jnp.arange(ETA, dtype=jnp.float32) + 0.5) / ETA
    shape_sum = 1.0 / normalized_blend_variance - 1.0
    alpha = average_blend_fraction * shape_sum
    beta_b = (1.0 - average_blend_fraction) * shape_sum
    logits = (alpha - 1.0)[..., None] * jnp.log(points) + (beta_b - 1.0)[..., None] * jnp.log(1.0 - points)
    return jax.nn.softmax(logits, axis=-1)


def lap_mixture(field):
    bordered_grid = jnp.concatenate([field[..., :1], field, field[..., -1:]], axis=-1)
    return bordered_grid[..., 2:] - 2.0 * field + bordered_grid[..., :-2]


def coarse_advance(fluid_condition, nearby, scalar_decay_speed, counts, chemical_coupling, turns):
    fluid_condition = fluid_condition + coupling * jnp.sum(nearby - fluid_condition[:, None], axis=1)
    fraction = 1.0 / counts.astype(jnp.float32)

    def substep(index, current):
        source = jnp.einsum("st,ctk->csk", chemical_coupling, jnp.tanh(current), precision=lax.Precision.HIGHEST)
        update = fraction[:, None, None] * (mixing_rate * scalar_decay_speed[:, None, :] * lap_mixture(current) + react_rate * source)
        return jnp.where((index < counts)[:, None, None], current + update, current)

    return lax.fori_loop(0, turns, substep, fluid_condition)


def small_volume_accumulations(average_blend_fraction, normalized_blend_variance, small_volume_mass, bare_scalar_decay, thermal_grid, parent_block, block_numbers):
    def attach_line(overall_aggregate, row):
        zm_row, zs_row, wt_row, cb_row, tp_row, ids_row = row
        tabulated_values = beta_table(zm_row, zs_row).reshape(-1, ETA)
        weighted = wt_row.reshape(-1, 1) * tabulated_values
        scalar_decay_speed = (cb_row * (1.0 + 0.5 * jnp.tanh(tp_row))).reshape(-1, 1)
        values = jnp.stack([weighted, weighted * scalar_decay_speed], axis=1)
        return overall_aggregate + jax.ops.segment_sum(values, ids_row.reshape(-1), num_segments=block_numbers), None

    first_shift_amount = jnp.zeros((block_numbers, 2, ETA), jnp.float32)
    overall_aggregate, discarded_quantity = lax.scan(attach_line, first_shift_amount, (average_blend_fraction, normalized_blend_variance, small_volume_mass, bare_scalar_decay, thermal_grid, parent_block))
    return overall_aggregate


def reverse_quadrature(average_blend_fraction, normalized_blend_variance, parent_block, blend_block_number):
    def one_row(row):
        zm_row, zs_row, ids_row = row
        tabulated_values = beta_table(zm_row, zs_row)
        return jnp.sum(tabulated_values * blend_block_number[ids_row], axis=-1)

    return lax.map(one_row, (average_blend_fraction, normalized_blend_variance, parent_block))


def small_grid_renewal(thermal_grid, small_grid_thermal):
    bordered_grid = jnp.pad(thermal_grid, 1)
    nearby_blocks = bordered_grid[2:, 1:-1, 1:-1] + bordered_grid[:-2, 1:-1, 1:-1]
    nearby_blocks = nearby_blocks + bordered_grid[1:-1, 2:, 1:-1] + bordered_grid[1:-1, :-2, 1:-1]
    nearby_blocks = nearby_blocks + bordered_grid[1:-1, 1:-1, 2:] + bordered_grid[1:-1, 1:-1, :-2]
    return thermal_grid + thermal_diffusion * (nearby_blocks - 6.0 * thermal_grid) + damping_contribution * (small_grid_thermal - thermal_grid)


def reference(thermal_grid, average_blend_fraction, normalized_blend_variance, small_volume_mass, bare_scalar_decay, parent_block, species_given_block, block_position, face_partners, reaction_increments, chemical_coupling, species_thermal_weight):
    position_block_map = jnp.argsort(block_position).astype(jnp.int32)
    near_slot = block_position[face_partners[position_block_map]]
    counts = reaction_increments[position_block_map] + 1
    fluid_condition = species_given_block
    for turn in range(STEPS):
        local_aggregates = small_volume_accumulations(average_blend_fraction, normalized_blend_variance, small_volume_mass, bare_scalar_decay, thermal_grid, parent_block, BLOCK_COUNT)[position_block_map]
        cchi = (local_aggregates[:, 1] + prior_flux) / (local_aggregates[:, 0] + prior_weight)
        fluid_condition = coarse_advance(fluid_condition, fluid_condition[near_slot], cchi, counts, chemical_coupling, SUBMAX)
        reduced_thermal = jnp.einsum("s,csk->ck", species_thermal_weight, fluid_condition, precision=lax.Precision.HIGHEST)
        small_grid_thermal = reverse_quadrature(average_blend_fraction, normalized_blend_variance, parent_block, reduced_thermal[block_position])
        thermal_grid = small_grid_renewal(thermal_grid, small_grid_thermal)
    return fluid_condition, thermal_grid
```

```python
import functools

import jax
import jax.numpy as jnp
from jax import lax
from jax.experimental import pallas as pl
from jax.experimental.pallas import tpu as pltpu
from jax.sharding import PartitionSpec as P

ETA = 128
SPEC = 16
SUBMAX = 16
STEPS = 2
ROWS = 4
OWNED = 4

coupling = 0.05
mixing_rate = 0.2
react_rate = 0.5
prior_weight = 1.0
prior_flux = 0.5
thermal_diffusion = 0.1
damping_contribution = 0.3

MESH = pl.DeviceIdType.MESH
HIGHEST = lax.Precision.HIGHEST
NT = (((1,), (1,)), ((), ()))
f32, bf16, i32 = jnp.float32, jnp.bfloat16, jnp.int32


def kernel(
    gxn, gyn, xs, ys,
    thermal, mean, variance, mass, decay, parent, state0, position_row, chem, weight,
    position, partners, increments,
    species_out, thermal_out,
    ids, log_a, log_b, shape_a, shape_b, chi, grid, fine, table, table16, total,
    sent, got, theta, state, face_x, face_y, own_y,
    sums_send, sums_recv, theta_send, theta_recv, state_send, state_recv, halo_send, halo_recv,
):
    ndev = gxn * gyn
    blocks = ndev * OWNED
    rows = xs * ys
    turns = rows // ROWS
    pairs = gyn // 2
    gx, gy = lax.axis_index("gx"), lax.axis_index("gy")
    me = gx * gyn + gy
    core, pair = lax.rem(gy, 2), gy // 2

    def place(device):
        device = lax.rem(device + ndev, ndev)
        return (device // gyn, lax.rem(device, gyn))

    barrier = pltpu.get_barrier_semaphore()

    @pl.loop(1, ndev)
    def _(j):
        pl.semaphore_signal(barrier, inc=1, device_id=place(me + j), device_id_type=MESH)

    row = lax.broadcasted_iota(i32, (ndev * 8, blocks), 0)
    device = me - (row >> 3)
    slot = jnp.where(device < 0, device + ndev, device) * OWNED + (row & 3)
    hit = position_row[...] == slot
    cell = lax.broadcasted_iota(i32, (ndev * 8, blocks), 1).astype(f32)
    named = jnp.sum(jnp.where(hit, cell, 0.0), axis=1, keepdims=True).astype(i32)
    ids[...] = jnp.broadcast_to(named, (ndev * 8, 128)).reshape(ndev, 8, 128)

    points = (lax.broadcasted_iota(i32, (ETA, 128), 0).astype(f32) + 0.5) / ETA
    log_a[...] = jnp.log(points)
    log_b[...] = jnp.log(1.0 - points)
    shape_sum = 1.0 / variance[...] - 1.0
    shape_a[...] = mean[...] * shape_sum - 1.0
    shape_b[...] = (1.0 - mean[...]) * shape_sum - 1.0
    grid[...] = thermal[...]

    spread = (
        (lax.broadcasted_iota(i32, (OWNED * SPEC, SPEC), 0) & (SPEC - 1))
        == lax.broadcasted_iota(i32, (OWNED * SPEC, SPEC), 1)
    ).astype(f32)
    wide = jnp.dot(spread, chem[...], precision=HIGHEST, preferred_element_type=f32)
    wide = lax.dot_general(wide, spread, NT, precision=HIGHEST, preferred_element_type=f32)
    same = (lax.broadcasted_iota(i32, wide.shape, 0) >> 4) == (
        lax.broadcasted_iota(i32, wide.shape, 1) >> 4
    )
    wide = jnp.where(same, wide, 0.0)
    wide_high = wide.astype(bf16)
    wide_low = (wide - wide_high.astype(f32)).astype(bf16)
    chem_all = jnp.concatenate([wide_high, wide_low], axis=0)

    weights = lax.dot_general(
        jnp.broadcast_to(weight[...], (8, SPEC)), spread, NT,
        precision=HIGHEST, preferred_element_type=f32,
    )
    mine = (lax.broadcasted_iota(i32, weights.shape, 0) & 3) == (
        lax.broadcasted_iota(i32, weights.shape, 1) >> 4
    )
    weights = jnp.where(mine, weights, 0.0)

    pl.semaphore_wait(barrier, ndev - 1)

    pending = []

    def along_gx(turn, j):
        def block(x):
            return state.at[turn, core, pair, x]

        there = (lax.rem(gx + j, gxn), gy)
        here = block(gx)
        come = block(lax.rem(gx - j + gxn, gxn))
        sems = (state_send.at[turn, j - 1], state_recv.at[turn, j - 1])
        return (
            pltpu.make_async_remote_copy(here, here, *sems, there, MESH),
            pltpu.make_async_remote_copy(come, come, *sems, there, MESH),
        )

    def along_pair(turn, j):
        other = lax.rem(pair + j, pairs)
        there = (gx, other * 2 + core)
        here = state.at[turn, core, pair]
        come = state.at[turn, core, lax.rem(pair - j + pairs, pairs)]
        sems = (state_send.at[turn, gxn - 2 + j], state_recv.at[turn, gxn - 2 + j])
        return (
            pltpu.make_async_remote_copy(here, here, *sems, there, MESH),
            pltpu.make_async_remote_copy(come, come, *sems, there, MESH),
        )

    def across(turn):
        there = (gx, pair * 2 + 1 - core)
        here = state.at[turn, core]
        come = state.at[turn, 1 - core]
        last = gxn + pairs - 2
        sems = (state_send.at[turn, last], state_recv.at[turn, last])
        return (
            pltpu.make_async_remote_copy(here, here, *sems, there, MESH),
            pltpu.make_async_remote_copy(come, come, *sems, there, MESH),
        )

    def launch(copies):
        for out, _ in copies:
            out.start()
            pending.append(out)

    def arrive(copies):
        for _, come in copies:
            come.wait_recv()

    def leg(turn, which):
        if which == 0:
            return [along_gx(turn, j) for j in range(1, gxn)]
        if which == 1:
            return [along_pair(turn, j) for j in range(1, pairs)]
        return [across(turn)]

    def halo(turn):
        low = (lax.rem(gx - 1 + gxn, gxn), gy)
        high = (lax.rem(gx + 1, gxn), gy)
        left = (gx, lax.rem(gy - 1 + gyn, gyn))
        right = (gx, lax.rem(gy + 1, gyn))
        source = grid if turn else thermal
        first = source.at[pl.ds(0, ys)]
        last = source.at[pl.ds((xs - 1) * ys, ys)]
        ends = [
            (last, face_x.at[turn, 0], high),
            (first, face_x.at[turn, 1], low),
            (own_y.at[turn], face_y.at[turn, 0], right),
            (own_y.at[turn], face_y.at[turn, 1], left),
        ]
        copies = [
            pltpu.make_async_remote_copy(
                s, d, halo_send.at[turn, n], halo_recv.at[turn, n], there, MESH
            )
            for n, (s, d, there) in enumerate(ends)
        ]
        return [(c, c) for c in copies]

    def send_halo(turn):
        now = grid[...]
        own_y[turn] = jnp.concatenate(
            [now[x * ys : x * ys + 1] for x in range(xs)]
            + [now[x * ys + ys - 1 : (x + 1) * ys] for x in range(xs)],
            axis=0,
        )
        launch(halo(turn))

    def exchange(source, target, turn, sign, send, recv):
        @pl.loop(1, ndev)
        def _(j):
            pltpu.make_async_remote_copy(
                source(j), target.at[turn, j], send.at[turn], recv.at[turn],
                place(me + sign * j), MESH,
            ).start()

        rest = target.at[turn, pl.ds(1, ndev - 1)]
        whole = pltpu.make_async_remote_copy(
            rest, rest, send.at[turn], recv.at[turn], place(me + 1), MESH
        )
        pending.append(whole)
        whole.wait_recv()

    half_row = lax.broadcasted_iota(i32, (8, 128), 0) < 4

    def gather_row(r):
        here = mass[pl.ds(r, 1), :]
        both = jnp.where(half_row, here, here * chi[pl.ds(r, 1), :])
        chosen = jnp.where(parent[pl.ds(r, 1), :][None] == ids[...], both[None], 0.0)
        return chosen.reshape(ndev * 8, 128).astype(bf16)

    def add_up(i, chosen, values):
        total[...] += lax.dot_general(
            jnp.concatenate(chosen, axis=1), values, NT, preferred_element_type=f32
        )

    def first_turn(i, cells):
        chosen = []
        for n in range(ROWS):
            r = i * ROWS + n
            logits = shape_a[pl.ds(r, 1), :] * log_a[...] + shape_b[pl.ds(r, 1), :] * log_b[...]
            raised = jnp.exp(logits - jnp.max(logits, axis=0, keepdims=True))
            part = raised * (1.0 / jnp.sum(raised, axis=0, keepdims=True))
            table[i, :, n * 128 : (n + 1) * 128] = part
            table16[i, :, n * 128 : (n + 1) * 128] = part.astype(bf16)
            chosen.append(gather_row(r))
        add_up(i, chosen, table16[i])
        each = blocks // turns
        for n in range(each):
            c = i * each + n
            at = position[c]
            cells = tuple(
                jnp.where(at == me * OWNED + q, c, cells[q]) for q in range(OWNED)
            )
        return cells

    def second_turn(i, carry):
        add_up(i, [gather_row(i * ROWS + n) for n in range(ROWS)], table16[i])
        return carry

    def reduce_sums(turn):
        sent[turn] = total[...].reshape(ndev, 8, 128)
        exchange(lambda j: sent.at[turn, j], got, turn, -1, sums_send, sums_recv)
        return sent[turn, 0] + jnp.sum(got[turn, pl.ds(1, ndev - 1)], axis=0)

    def spread_rows(pieces):
        return jnp.concatenate(
            [jnp.broadcast_to(p, (SPEC, 128)) for p in pieces], axis=0
        )

    lane = lax.broadcasted_iota(i32, (OWNED * SPEC, 128), 1)

    def advance(turn, sums, cells):
        cchi = (sums[4:8] + prior_flux) / (sums[0:4] + prior_weight)
        cchi = spread_rows([cchi[q : q + 1] for q in range(OWNED)])
        counts = jnp.concatenate(
            [jnp.full((SPEC, 128), increments[cells[q]] + 1, i32) for q in range(OWNED)], axis=0
        )
        fraction = 1.0 / counts.astype(f32)
        mixed = fraction * mixing_rate * cchi
        reacted = fraction * react_rate
        parts = []
        for q in range(OWNED):
            around = None
            for j in range(6):
                near = position[partners[cells[q] * 6 + j]]
                d = near >> 2
                y = lax.rem(d, gyn)
                there = state[
                    turn, lax.rem(y, 2), y // 2, d // gyn, pl.ds((near & 3) * SPEC, SPEC), :
                ]
                around = there if around is None else around + there
            parts.append(around)
        around = jnp.concatenate(parts, axis=0)
        now = state0[...] if turn == 0 else species_out[...]
        now = now + coupling * (around - 6.0 * now)

        def substep(index, current):
            bent = jnp.tanh(current)
            high = bent.astype(bf16)
            low = (bent - high.astype(f32)).astype(bf16)
            source = jnp.dot(
                chem_all, jnp.concatenate([high, low], axis=1), preferred_element_type=f32
            )
            n = OWNED * SPEC
            source = source[:n, :128] + (source[:n, 128:] + source[n:, :128])
            left = jnp.where(lane == 0, current, pltpu.roll(current, 1, 1))
            right = jnp.where(lane == 127, current, pltpu.roll(current, 127, 1))
            update = mixed * (right - 2.0 * current + left) + reacted * source
            return jnp.where(index < counts, current + update, current)

        now = lax.fori_loop(0, SUBMAX, substep, now)
        species_out[...] = now
        theta[turn, 0] = jnp.dot(weights, now, precision=HIGHEST, preferred_element_type=f32)
        return now

    def refine(turn):
        exchange(lambda j: theta.at[turn, 0], theta, turn, 1, theta_send, theta_recv)
        whole = theta[turn]
        high = whole.astype(bf16).astype(f32)
        halves = jnp.where(half_row[None], high, whole - high).reshape(ndev * 8, 128)
        halves = halves.T.astype(bf16)

        def body(i, carry):
            picks = [
                jnp.where(parent[pl.ds(i * ROWS + n, 1), :][None] == ids[...], 1.0, 0.0)
                .reshape(ndev * 8, 128)
                .astype(bf16)
                for n in range(ROWS)
            ]
            picked = jnp.dot(
                halves, jnp.concatenate(picks, axis=1), preferred_element_type=f32
            )
            value = jnp.sum(table[i] * picked, axis=0, keepdims=True)
            for n in range(ROWS):
                fine[pl.ds(i * ROWS + n, 1), :] = value[:, n * 128 : (n + 1) * 128]
            return carry

        lax.fori_loop(0, turns, body, 0)

    def diffuse(turn):
        arrive(halo(turn))
        now = grid[...]
        zero = jnp.zeros((ys, 128), f32)
        low_x = jnp.where(gx == 0, zero, face_x[turn, 0])
        high_x = jnp.where(gx == gxn - 1, zero, face_x[turn, 1])
        around = jnp.concatenate([now[ys:], high_x], axis=0)
        around = around + jnp.concatenate([low_x, now[:-ys]], axis=0)
        low_y = jnp.where(gy == 0, 0.0, face_y[turn, 0])
        high_y = jnp.where(gy == gyn - 1, 0.0, face_y[turn, 1])
        low_y = jnp.concatenate(
            [jnp.broadcast_to(low_y[xs + x : xs + x + 1], (ys, 128)) for x in range(xs)], axis=0
        )
        high_y = jnp.concatenate(
            [jnp.broadcast_to(high_y[x : x + 1], (ys, 128)) for x in range(xs)], axis=0
        )
        y = lax.rem(lax.broadcasted_iota(i32, (rows, 128), 0), ys)
        around = around + jnp.where(y == ys - 1, high_y, pltpu.roll(now, rows - 1, 0))
        around = around + jnp.where(y == 0, low_y, pltpu.roll(now, 1, 0))
        z = lax.broadcasted_iota(i32, (rows, 128), 1)
        around = around + jnp.where(z == 127, 0.0, pltpu.roll(now, 127, 1))
        around = around + jnp.where(z == 0, 0.0, pltpu.roll(now, 1, 1))
        return (
            now
            + thermal_diffusion * (around - 6.0 * now)
            + damping_contribution * (fine[...] - now)
        )

    def dissipate():
        chi[...] = decay[...] * (1.0 + 0.5 * jnp.tanh(grid[...]))

    state[0, core, pair, gx] = state0[...]
    launch(leg(0, 0))
    send_halo(0)
    dissipate()
    total[...] = jnp.zeros_like(total)
    cells = (jnp.int32(0),) * OWNED
    cells = lax.fori_loop(0, turns // 2, first_turn, cells)
    arrive(leg(0, 0))
    launch(leg(0, 1))
    cells = lax.fori_loop(turns // 2, turns, first_turn, cells)
    arrive(leg(0, 1))
    launch(leg(0, 2))
    sums = reduce_sums(0)
    arrive(leg(0, 2))
    now = advance(0, sums, cells)
    state[1, core, pair, gx] = now
    refine(0)
    launch(leg(1, 0))
    after = diffuse(0)
    grid[...] = after

    send_halo(1)
    dissipate()
    arrive(leg(1, 0))
    launch(leg(1, 1))
    total[...] = jnp.zeros_like(total)
    lax.fori_loop(0, turns, second_turn, 0)
    arrive(leg(1, 1))
    launch(leg(1, 2))
    sums = reduce_sums(1)
    arrive(leg(1, 2))
    advance(1, sums, cells)
    refine(1)
    thermal_out[...] = diffuse(1)

    for copy in pending:
        copy.wait_send()


def shards(
    thermal_grid,
    average_blend_fraction,
    normalized_blend_variance,
    small_volume_mass,
    bare_scalar_decay,
    parent_block,
    species_given_block,
    block_position,
    face_partners,
    reaction_increments,
    chemical_coupling,
    species_thermal_weight,
):
    gxn, gyn = lax.axis_size("gx"), lax.axis_size("gy")
    ndev = gxn * gyn
    blocks = block_position.shape[0]
    xs, ys, zs = thermal_grid.shape
    rows = xs * ys
    turns = rows // ROWS
    assert blocks == ndev * OWNED and zs == 128 and rows % (2 * ROWS) == 0
    legs = gxn - 1 + gyn // 2 - 1 + 1
    vmem = pl.BlockSpec(memory_space=pltpu.VMEM)
    smem = pl.BlockSpec(memory_space=pltpu.SMEM)
    dma = pltpu.SemaphoreType.DMA
    species, thermal = pl.pallas_call(
        functools.partial(kernel, gxn, gyn, xs, ys),
        out_shape=(
            jax.ShapeDtypeStruct((OWNED * SPEC, ETA), f32),
            jax.ShapeDtypeStruct((rows, zs), f32),
        ),
        in_specs=[vmem] * 10 + [smem] * 3,
        out_specs=(vmem, vmem),
        scratch_shapes=[
            pltpu.VMEM((ndev, 8, 128), i32),
            pltpu.VMEM((ETA, 128), f32),
            pltpu.VMEM((ETA, 128), f32),
            pltpu.VMEM((rows, zs), f32),
            pltpu.VMEM((rows, zs), f32),
            pltpu.VMEM((rows, zs), f32),
            pltpu.VMEM((rows, zs), f32),
            pltpu.VMEM((rows, zs), f32),
            pltpu.VMEM((turns, ETA, ROWS * 128), f32),
            pltpu.VMEM((turns, ETA, ROWS * 128), bf16),
            pltpu.VMEM((ndev * 8, ETA), f32),
            pltpu.VMEM((STEPS, ndev, 8, ETA), f32),
            pltpu.VMEM((STEPS, ndev, 8, ETA), f32),
            pltpu.VMEM((STEPS, ndev, 8, ETA), f32),
            pltpu.VMEM((STEPS, 2, gyn // 2, gxn, OWNED * SPEC, ETA), f32),
            pltpu.VMEM((STEPS, 2, ys, zs), f32),
            pltpu.VMEM((STEPS, 2, 2 * xs, zs), f32),
            pltpu.VMEM((STEPS, 2 * xs, zs), f32),
            dma((STEPS,)),
            dma((STEPS,)),
            dma((STEPS,)),
            dma((STEPS,)),
            dma((STEPS, legs)),
            dma((STEPS, legs)),
            dma((STEPS, 4)),
            dma((STEPS, 4)),
        ],
        compiler_params=pltpu.CompilerParams(
            collective_id=0, has_side_effects=True, vmem_limit_bytes=48 * 1024 * 1024
        ),
    )(
        thermal_grid.reshape(rows, zs),
        average_blend_fraction.reshape(rows, zs),
        normalized_blend_variance.reshape(rows, zs),
        small_volume_mass.reshape(rows, zs),
        bare_scalar_decay.reshape(rows, zs),
        parent_block.reshape(rows, zs),
        species_given_block.reshape(OWNED * SPEC, ETA),
        block_position.reshape(1, blocks),
        chemical_coupling,
        species_thermal_weight.reshape(1, SPEC),
        block_position,
        face_partners.reshape(-1),
        reaction_increments,
    )
    return (species.reshape(OWNED, SPEC, ETA), thermal.reshape(xs, ys, zs))


def solution(mesh):
    fine = P("gx", "gy", None)
    return jax.shard_map(
        shards,
        mesh=mesh,
        in_specs=(fine,) * 6 + (P(("gx", "gy"), None, None),) + (P(),) * 5,
        out_specs=(P(("gx", "gy"), None, None), fine),
        check_vma=False,
    )
```

```python
import functools

import jax
import jax.numpy as jnp
from jax import lax
from jax.experimental import pallas as pl
from jax.experimental.pallas import tpu as pltpu
from jax.sharding import PartitionSpec as P

ETA = 128
SPEC = 16
SUBMAX = 16
STEPS = 2
ROWS = 8
OWNED = 4
NAMED = 48

coupling = 0.05
mixing_rate = 0.2
react_rate = 0.5
prior_weight = 1.0
prior_flux = 0.5
thermal_diffusion = 0.1
damping_contribution = 0.3

MESH = pl.DeviceIdType.MESH
HIGHEST = lax.Precision.HIGHEST
NT = (((1,), (1,)), ((), ()))
f32, bf16, i32 = jnp.float32, jnp.bfloat16, jnp.int32


def kernel(
    gxn, gyn, xs, ys,
    thermal_in, mean_in, variance_in, mass_in, decay_in, parent_in, state0_in, position_row_in,
    chem_in, weight_in, position_in, partners_in, increments_in,
    species_out, thermal_out,
    thermal, mean, variance, mass, decay, parent, state0, position_row, chem, weight,
    position, partners, increments, load,
    ids, names, names_row, bent_rows, columns, weights_known, log_a, log_b, shape_a, shape_b, chi, grid, fine, table, table16, total,
    sent, got, theta, state, face_x, face_y, own_y,
    sums_send, sums_recv, theta_send, theta_recv, state_send, state_recv, halo_send, halo_recv,
):
    ndev = gxn * gyn
    blocks = ndev * OWNED
    rows = xs * ys
    turns = rows // ROWS
    pairs = gyn // 2
    gx, gy = lax.axis_index("gx"), lax.axis_index("gy")
    me = gx * gyn + gy
    core, pair = lax.rem(gy, 2), gy // 2

    def place(device):
        device = lax.rem(device + ndev, ndev)
        return (device // gyn, lax.rem(device, gyn))

    barrier = pltpu.get_barrier_semaphore()

    @pl.loop(1, ndev)
    def _(j):
        pl.semaphore_signal(barrier, inc=1, device_id=place(me + j), device_id_type=MESH)

    loads = [
        pltpu.make_async_copy(source, target, load.at[n])
        for n, (source, target) in enumerate((
            (position_row_in, position_row), (parent_in, parent), (variance_in, variance),
            (mean_in, mean), (thermal_in, thermal), (mass_in, mass), (decay_in, decay),
            (state0_in, state0), (chem_in, chem), (weight_in, weight),
            (position_in, position), (partners_in, partners), (increments_in, increments),
        ))
    ]
    for copy in loads:
        copy.start()
    for copy in loads:
        copy.wait()

    row = lax.broadcasted_iota(i32, (ndev * 8, blocks), 0)
    device = me - (row >> 3)
    slot = jnp.where(device < 0, device + ndev, device) * OWNED + (row & 3)
    hit = position_row[...] == slot
    cell = lax.broadcasted_iota(i32, (ndev * 8, blocks), 1).astype(f32)
    named = jnp.sum(jnp.where(hit, cell, 0.0), axis=1, keepdims=True).astype(i32)
    ids[...] = jnp.broadcast_to(named, (ndev * 8, 128))

    coarse = lax.broadcasted_iota(i32, (blocks, 128), 0)

    def look(i, seen):
        for n in range(8):
            seen = jnp.where(parent[pl.ds(i * 8 + n, 1), :] == coarse, 1.0, seen)
        return seen

    seen = lax.fori_loop(0, rows // 8, look, jnp.zeros((blocks, 128), f32))
    seen = jnp.broadcast_to(jnp.max(seen, axis=1, keepdims=True), (blocks, 128))
    below = (
        lax.broadcasted_iota(i32, (blocks, blocks), 1)
        < lax.broadcasted_iota(i32, (blocks, blocks), 0)
    )
    rank = jnp.dot(
        jnp.where(below, 1.0, 0.0).astype(bf16), seen.astype(bf16), preferred_element_type=f32
    )
    lanes = lax.broadcasted_iota(i32, (1, 128), 1)
    wanted = jnp.where(lanes < NAMED, lanes, jnp.where(lanes < 2 * NAMED, lanes - NAMED, -1))
    match = (rank == wanted.astype(f32)) & (seen > 0.0)
    list_row = jnp.sum(jnp.where(match, coarse.astype(f32) + 1.0, 0.0), axis=0, keepdims=True) - 1.0
    names_row[...] = jnp.broadcast_to(list_row, (8, 128)).astype(i32)
    names[...] = jnp.broadcast_to(list_row, (128, 128)).T[:NAMED].astype(i32)

    points = (lax.broadcasted_iota(i32, (ETA, 128), 0).astype(f32) + 0.5) / ETA
    log_a[...] = jnp.log(points)
    log_b[...] = jnp.log(1.0 - points)
    shape_sum = 1.0 / variance[...] - 1.0
    shape_a[...] = mean[...] * shape_sum - 1.0
    shape_b[...] = (1.0 - mean[...]) * shape_sum - 1.0
    grid[...] = thermal[...]

    spread = (
        (lax.broadcasted_iota(i32, (OWNED * SPEC, SPEC), 0) & (SPEC - 1))
        == lax.broadcasted_iota(i32, (OWNED * SPEC, SPEC), 1)
    ).astype(f32)
    for t in range(SPEC):
        columns[t] = jnp.broadcast_to(chem[:, t : t + 1], (SPEC, 128))

    weights = lax.dot_general(
        jnp.broadcast_to(weight[...], (8, SPEC)), spread, NT,
        precision=HIGHEST, preferred_element_type=f32,
    )
    mine = (lax.broadcasted_iota(i32, weights.shape, 0) & 3) == (
        lax.broadcasted_iota(i32, weights.shape, 1) >> 4
    )
    weights = jnp.where(mine, weights, 0.0)

    pl.semaphore_wait(barrier, ndev - 1)

    pending = []

    def along_gx(turn, j):
        def block(x):
            return state.at[turn, core, pair, x]

        there = (lax.rem(gx + j, gxn), gy)
        here = block(gx)
        come = block(lax.rem(gx - j + gxn, gxn))
        sems = (state_send.at[turn, j - 1], state_recv.at[turn, j - 1])
        return (
            pltpu.make_async_remote_copy(here, here, *sems, there, MESH),
            pltpu.make_async_remote_copy(come, come, *sems, there, MESH),
        )

    def along_pair(turn, j):
        other = lax.rem(pair + j, pairs)
        there = (gx, other * 2 + core)
        here = state.at[turn, core, pair]
        come = state.at[turn, core, lax.rem(pair - j + pairs, pairs)]
        sems = (state_send.at[turn, gxn - 2 + j], state_recv.at[turn, gxn - 2 + j])
        return (
            pltpu.make_async_remote_copy(here, here, *sems, there, MESH),
            pltpu.make_async_remote_copy(come, come, *sems, there, MESH),
        )

    def across(turn):
        there = (gx, pair * 2 + 1 - core)
        here = state.at[turn, core]
        come = state.at[turn, 1 - core]
        last = gxn + pairs - 2
        sems = (state_send.at[turn, last], state_recv.at[turn, last])
        return (
            pltpu.make_async_remote_copy(here, here, *sems, there, MESH),
            pltpu.make_async_remote_copy(come, come, *sems, there, MESH),
        )

    def launch(copies):
        for out, _ in copies:
            out.start()
            pending.append(out)

    def arrive(copies):
        for _, come in copies:
            come.wait_recv()

    def leg(turn, which):
        if which == 0:
            return [along_gx(turn, j) for j in range(1, gxn)]
        if which == 1:
            return [along_pair(turn, j) for j in range(1, pairs)]
        return [across(turn)]

    def halo(turn):
        low = (lax.rem(gx - 1 + gxn, gxn), gy)
        high = (lax.rem(gx + 1, gxn), gy)
        left = (gx, lax.rem(gy - 1 + gyn, gyn))
        right = (gx, lax.rem(gy + 1, gyn))
        source = grid if turn else thermal
        first = source.at[pl.ds(0, ys)]
        last = source.at[pl.ds((xs - 1) * ys, ys)]
        ends = [
            (last, face_x.at[turn, 0], high),
            (first, face_x.at[turn, 1], low),
            (own_y.at[turn], face_y.at[turn, 0], right),
            (own_y.at[turn], face_y.at[turn, 1], left),
        ]
        copies = [
            pltpu.make_async_remote_copy(
                s, d, halo_send.at[turn, n], halo_recv.at[turn, n], there, MESH
            )
            for n, (s, d, there) in enumerate(ends)
        ]
        return [(c, c) for c in copies]

    def send_halo(turn):
        now = grid[...]
        own_y[turn] = jnp.concatenate(
            [now[x * ys : x * ys + 1] for x in range(xs)]
            + [now[x * ys + ys - 1 : (x + 1) * ys] for x in range(xs)],
            axis=0,
        )
        launch(halo(turn))

    def exchange(source, target, turn, sign, send, recv):
        @pl.loop(1, ndev)
        def _(j):
            pltpu.make_async_remote_copy(
                source(j), target.at[turn, j], send.at[turn], recv.at[turn],
                place(me + sign * j), MESH,
            ).start()

        rest = target.at[turn, pl.ds(1, ndev - 1)]
        whole = pltpu.make_async_remote_copy(
            rest, rest, send.at[turn], recv.at[turn], place(me + 1), MESH
        )
        pending.append(whole)
        whole.wait_recv()

    half_row = lax.broadcasted_iota(i32, (8, 128), 0) < 4
    upper = (lax.broadcasted_iota(i32, (ndev * 8, 128), 0) & 4) == 0

    def split(values):
        high = values.astype(bf16)
        return [high, (values - high.astype(f32)).astype(bf16)]

    def same_cell():
        return ids[...] == names_row[0:1, :]

    def hits(r):
        return parent[pl.ds(r, 1), :] == names[...]

    def gather_row(r, first):
        hit = hits(r)
        here = mass[pl.ds(r, 1), :]
        parts = [jnp.where(hit, here * chi[pl.ds(r, 1), :], 0.0).astype(bf16)]
        if first:
            parts = [jnp.where(hit, here, 0.0).astype(bf16)] + parts
        return jnp.concatenate(parts, axis=0)

    def add_up(chosen, values):
        chosen = jnp.concatenate(chosen, axis=1)
        count = chosen.shape[0]
        total[128 - 32 - count : 96] += lax.dot_general(
            chosen, values, NT, preferred_element_type=f32
        )

    def first_turn(i, cells):
        chosen = []
        for n in range(ROWS):
            r = i * ROWS + n
            logits = shape_a[pl.ds(r, 1), :] * log_a[...] + shape_b[pl.ds(r, 1), :] * log_b[...]
            raised = jnp.exp(logits - jnp.max(logits, axis=0, keepdims=True))
            part = raised * (1.0 / jnp.sum(raised, axis=0, keepdims=True))
            table[i, :, n * 128 : (n + 1) * 128] = part
            table16[i, :, n * 128 : (n + 1) * 128] = part.astype(bf16)
            chosen.append(gather_row(r, True))
        add_up(chosen, table16[i])
        each = blocks // turns
        for n in range(each):
            c = i * each + n
            at = position[c]
            cells = tuple(
                jnp.where(at == me * OWNED + q, c, cells[q]) for q in range(OWNED)
            )
        return cells

    def second_turn(i, carry):
        add_up([gather_row(i * ROWS + n, False) for n in range(ROWS)], table16[i])
        return carry

    def reduce_sums(turn):
        lane_low = lax.broadcasted_iota(i32, (ndev * 8, 128), 1) < NAMED
        pick = jnp.where(same_cell() & (lane_low == upper), 1.0, 0.0).astype(bf16)
        sums = jnp.dot(
            jnp.concatenate([pick, pick], axis=1),
            jnp.concatenate(split(total[...]), axis=0),
            preferred_element_type=f32,
        )
        sent[turn] = sums.reshape(ndev, 8, 128)
        exchange(lambda j: sent.at[turn, j], got, turn, -1, sums_send, sums_recv)
        return sent[turn, 0] + jnp.sum(got[turn, pl.ds(1, ndev - 1)], axis=0)

    def spread_rows(pieces):
        return jnp.concatenate(
            [jnp.broadcast_to(p, (SPEC, 128)) for p in pieces], axis=0
        )

    lane = lax.broadcasted_iota(i32, (OWNED * SPEC, 128), 1)

    def advance(turn, sums, cells):
        if turn == 0:
            weights_known[...] = sums
        cchi = (sums[4:8] + prior_flux) / (weights_known[0:4] + prior_weight)
        cchi = spread_rows([cchi[q : q + 1] for q in range(OWNED)])
        counts = jnp.concatenate(
            [jnp.full((SPEC, 128), increments[cells[q]] + 1, i32) for q in range(OWNED)], axis=0
        )
        fraction = 1.0 / counts.astype(f32)
        mixed = fraction * mixing_rate * cchi
        reacted = fraction * react_rate
        parts = []
        for q in range(OWNED):
            around = None
            for j in range(6):
                near = position[partners[cells[q], j]]
                d = near >> 2
                y = lax.rem(d, gyn)
                there = state[
                    turn, lax.rem(y, 2), y // 2, d // gyn, pl.ds((near & 3) * SPEC, SPEC), :
                ]
                around = there if around is None else around + there
            parts.append(around)
        around = jnp.concatenate(parts, axis=0)
        now = state0[...] if turn == 0 else species_out[...]
        now = now + coupling * (around - 6.0 * now)

        def substep(index, current):
            bent_rows[...] = jnp.tanh(current)
            sources = [None] * OWNED
            for t in range(SPEC):
                column = columns[t]
                for q in range(OWNED):
                    term = column * bent_rows[q * SPEC + t : q * SPEC + t + 1, :]
                    sources[q] = term if t == 0 else sources[q] + term
            source = jnp.concatenate(sources, axis=0)
            left = jnp.where(lane == 0, current, pltpu.roll(current, 1, 1))
            right = jnp.where(lane == 127, current, pltpu.roll(current, 127, 1))
            update = mixed * (right - 2.0 * current + left) + reacted * source
            return jnp.where(index < counts, current + update, current)

        now = lax.fori_loop(0, SUBMAX, substep, now)
        species_out[...] = now
        theta[turn, 0] = jnp.dot(weights, now, precision=HIGHEST, preferred_element_type=f32)
        return now

    def refine(turn):
        exchange(lambda j: theta.at[turn, 0], theta, turn, 1, theta_send, theta_recv)
        if turn == 0:
            launch(leg(1, 0))
        flat = theta[turn].reshape(ndev * 8, 128).T
        pick = jnp.where(same_cell() & upper, 1.0, 0.0).astype(bf16)
        whole = jnp.dot(
            jnp.concatenate(split(flat), axis=1),
            jnp.concatenate([pick, pick], axis=0),
            preferred_element_type=f32,
        )
        high = whole.astype(bf16).astype(f32)
        lanes_all = lax.broadcasted_iota(i32, (ETA, 128), 1)
        halves = jnp.where(lanes_all < NAMED, high, whole - high).astype(bf16)
        blank = jnp.zeros((128 - 2 * NAMED, 128), bf16)

        def body(i, carry):
            picks = []
            for n in range(ROWS):
                hit = jnp.where(hits(i * ROWS + n), 1.0, 0.0).astype(bf16)
                picks.append(jnp.concatenate([hit, hit, blank], axis=0))
            picked = jnp.dot(
                halves, jnp.concatenate(picks, axis=1), preferred_element_type=f32
            )
            value = jnp.sum(table[i] * picked, axis=0, keepdims=True)
            for n in range(ROWS):
                fine[pl.ds(i * ROWS + n, 1), :] = value[:, n * 128 : (n + 1) * 128]
            return carry

        lax.fori_loop(0, turns, body, 0)

    def diffuse(turn):
        arrive(halo(turn))
        now = grid[...]
        zero = jnp.zeros((ys, 128), f32)
        low_x = jnp.where(gx == 0, zero, face_x[turn, 0])
        high_x = jnp.where(gx == gxn - 1, zero, face_x[turn, 1])
        around = jnp.concatenate([now[ys:], high_x], axis=0)
        around = around + jnp.concatenate([low_x, now[:-ys]], axis=0)
        low_y = jnp.where(gy == 0, 0.0, face_y[turn, 0])
        high_y = jnp.where(gy == gyn - 1, 0.0, face_y[turn, 1])
        low_y = jnp.concatenate(
            [jnp.broadcast_to(low_y[xs + x : xs + x + 1], (ys, 128)) for x in range(xs)], axis=0
        )
        high_y = jnp.concatenate(
            [jnp.broadcast_to(high_y[x : x + 1], (ys, 128)) for x in range(xs)], axis=0
        )
        y = lax.rem(lax.broadcasted_iota(i32, (rows, 128), 0), ys)
        around = around + jnp.where(y == ys - 1, high_y, pltpu.roll(now, rows - 1, 0))
        around = around + jnp.where(y == 0, low_y, pltpu.roll(now, 1, 0))
        z = lax.broadcasted_iota(i32, (rows, 128), 1)
        around = around + jnp.where(z == 127, 0.0, pltpu.roll(now, 127, 1))
        around = around + jnp.where(z == 0, 0.0, pltpu.roll(now, 1, 1))
        return (
            now
            + thermal_diffusion * (around - 6.0 * now)
            + damping_contribution * (fine[...] - now)
        )

    def dissipate():
        chi[...] = decay[...] * (1.0 + 0.5 * jnp.tanh(grid[...]))

    state[0, core, pair, gx] = state0[...]
    launch(leg(0, 0))
    send_halo(0)
    dissipate()
    total[...] = jnp.zeros_like(total)
    cells = (jnp.int32(0),) * OWNED
    cells = lax.fori_loop(0, turns // 2, first_turn, cells)
    arrive(leg(0, 0))
    launch(leg(0, 1))
    cells = lax.fori_loop(turns // 2, turns, first_turn, cells)
    arrive(leg(0, 1))
    launch(leg(0, 2))
    sums = reduce_sums(0)
    arrive(leg(0, 2))
    now = advance(0, sums, cells)
    state[1, core, pair, gx] = now
    refine(0)
    arrive(leg(1, 0))
    launch(leg(1, 1))
    grid[...] = diffuse(0)

    send_halo(1)
    dissipate()
    total[...] = jnp.zeros_like(total)
    lax.fori_loop(0, turns, second_turn, 0)
    arrive(leg(1, 1))
    launch(leg(1, 2))
    sums = reduce_sums(1)
    arrive(leg(1, 2))
    advance(1, sums, cells)
    refine(1)
    thermal_out[...] = diffuse(1)

    for copy in pending:
        copy.wait_send()


def shards(
    thermal_grid,
    average_blend_fraction,
    normalized_blend_variance,
    small_volume_mass,
    bare_scalar_decay,
    parent_block,
    species_given_block,
    block_position,
    face_partners,
    reaction_increments,
    chemical_coupling,
    species_thermal_weight,
):
    gxn, gyn = lax.axis_size("gx"), lax.axis_size("gy")
    ndev = gxn * gyn
    blocks = block_position.shape[0]
    xs, ys, zs = thermal_grid.shape
    rows = xs * ys
    turns = rows // ROWS
    assert blocks == ndev * OWNED and zs == 128 and rows % (2 * ROWS) == 0
    legs = gxn - 1 + gyn // 2 - 1 + 1
    vmem = pl.BlockSpec(memory_space=pltpu.VMEM)
    dma = pltpu.SemaphoreType.DMA
    species, thermal = pl.pallas_call(
        functools.partial(kernel, gxn, gyn, xs, ys),
        out_shape=(
            jax.ShapeDtypeStruct((OWNED * SPEC, ETA), f32),
            jax.ShapeDtypeStruct((rows, zs), f32),
        ),
        in_specs=[pl.BlockSpec(memory_space=pltpu.HBM)] * 13,
        out_specs=(vmem, vmem),
        scratch_shapes=[
            *[pltpu.VMEM((rows, zs), f32)] * 5,
            pltpu.VMEM((rows, zs), i32),
            pltpu.VMEM((OWNED * SPEC, ETA), f32),
            pltpu.VMEM((1, blocks), i32),
            pltpu.VMEM((SPEC, SPEC), f32),
            pltpu.VMEM((1, SPEC), f32),
            pltpu.SMEM((blocks,), i32),
            pltpu.SMEM((blocks, 6), i32),
            pltpu.SMEM((blocks,), i32),
            dma((13,)),
            pltpu.VMEM((ndev * 8, 128), i32),
            pltpu.VMEM((NAMED, 128), i32),
            pltpu.VMEM((8, 128), i32),
            pltpu.VMEM((OWNED * SPEC, ETA), f32),
            pltpu.VMEM((SPEC, SPEC, ETA), f32),
            pltpu.VMEM((8, ETA), f32),
            pltpu.VMEM((ETA, 128), f32),
            pltpu.VMEM((ETA, 128), f32),
            pltpu.VMEM((rows, zs), f32),
            pltpu.VMEM((rows, zs), f32),
            pltpu.VMEM((rows, zs), f32),
            pltpu.VMEM((rows, zs), f32),
            pltpu.VMEM((rows, zs), f32),
            pltpu.VMEM((turns, ETA, ROWS * 128), f32),
            pltpu.VMEM((turns, ETA, ROWS * 128), bf16),
            pltpu.VMEM((128, ETA), f32),
            pltpu.VMEM((STEPS, ndev, 8, ETA), f32),
            pltpu.VMEM((STEPS, ndev, 8, ETA), f32),
            pltpu.VMEM((STEPS, ndev, 8, ETA), f32),
            pltpu.VMEM((STEPS, 2, gyn // 2, gxn, OWNED * SPEC, ETA), f32),
            pltpu.VMEM((STEPS, 2, ys, zs), f32),
            pltpu.VMEM((STEPS, 2, 2 * xs, zs), f32),
            pltpu.VMEM((STEPS, 2 * xs, zs), f32),
            dma((STEPS,)),
            dma((STEPS,)),
            dma((STEPS,)),
            dma((STEPS,)),
            dma((STEPS, legs)),
            dma((STEPS, legs)),
            dma((STEPS, 4)),
            dma((STEPS, 4)),
        ],
        compiler_params=pltpu.CompilerParams(
            collective_id=0, has_side_effects=True, vmem_limit_bytes=48 * 1024 * 1024
        ),
    )(
        thermal_grid.reshape(rows, zs),
        average_blend_fraction.reshape(rows, zs),
        normalized_blend_variance.reshape(rows, zs),
        small_volume_mass.reshape(rows, zs),
        bare_scalar_decay.reshape(rows, zs),
        parent_block.reshape(rows, zs),
        species_given_block.reshape(OWNED * SPEC, ETA),
        block_position.reshape(1, blocks),
        chemical_coupling,
        species_thermal_weight.reshape(1, SPEC),
        block_position,
        face_partners,
        reaction_increments,
    )
    return (species.reshape(OWNED, SPEC, ETA), thermal.reshape(xs, ys, zs))


def solution(mesh):
    fine = P("gx", "gy", None)
    return jax.shard_map(
        shards,
        mesh=mesh,
        in_specs=(fine,) * 6 + (P(("gx", "gy"), None, None),) + (P(),) * 5,
        out_specs=(P(("gx", "gy"), None, None), fine),
        check_vma=False,
    )
```

```python
import functools

import jax
import jax.numpy as jnp
from jax import lax
from jax.experimental import pallas as pl
from jax.experimental.pallas import tpu as pltpu
from jax.sharding import PartitionSpec as P

ETA = 128
SPEC = 16
SUBMAX = 16
STEPS = 2
ROWS = 8
OWNED = 4
NAMED = 48

coupling = 0.05
mixing_rate = 0.2
react_rate = 0.5
prior_weight = 1.0
prior_flux = 0.5
thermal_diffusion = 0.1
damping_contribution = 0.3

MESH = pl.DeviceIdType.MESH
HIGHEST = lax.Precision.HIGHEST
NT = (((1,), (1,)), ((), ()))
f32, bf16, i32 = jnp.float32, jnp.bfloat16, jnp.int32


def kernel(
    gxn, gyn, xs, ys,
    thermal_in, mean_in, variance_in, mass_in, decay_in, parent_in, state0_in, position_row_in,
    chem_in, weight_in, position_in, partners_in, increments_in,
    species_out, thermal_out,
    thermal, mean, variance, mass, decay, parent, state0, position_row, chem, weight,
    position, partners, increments, load,
    ids, names, names_row, bent_rows, columns, weights_known, log_a, log_b, shape_a, shape_b, chi, grid, fine, table, table16, total,
    known, next_now, next_mixed, next_reacted, next_counts,
    sent, got, theta, state, face_x, face_y, own_y,
    sums_send, sums_recv, known_send, known_recv, theta_send, theta_recv, state_send, state_recv, halo_send, halo_recv,
):
    ndev = gxn * gyn
    blocks = ndev * OWNED
    rows = xs * ys
    turns = rows // ROWS
    xn = gyn // 2
    yn = xn if gxn % xn == 0 else 1
    zn = gxn // yn
    gx, gy = lax.axis_index("gx"), lax.axis_index("gy")
    me = gx * gyn + gy
    core, x = gy & 1, gy >> 1
    y, z = lax.rem(gx, yn), gx // yn

    def place(device):
        device = lax.rem(device + ndev, ndev)
        return (device // gyn, lax.rem(device, gyn))

    barrier = pltpu.get_barrier_semaphore()

    @pl.loop(1, ndev)
    def _(j):
        pl.semaphore_signal(barrier, inc=1, device_id=place(me + j), device_id_type=MESH)

    loads = [
        pltpu.make_async_copy(source, target, load.at[n])
        for n, (source, target) in enumerate((
            (position_row_in, position_row), (parent_in, parent), (variance_in, variance),
            (mean_in, mean), (thermal_in, thermal), (mass_in, mass), (decay_in, decay),
            (state0_in, state0), (chem_in, chem), (weight_in, weight),
            (position_in, position), (partners_in, partners), (increments_in, increments),
        ))
    ]
    for copy in loads:
        copy.start()
    for copy in loads:
        copy.wait()

    row = lax.broadcasted_iota(i32, (ndev * 8, blocks), 0)
    device = me - (row >> 3)
    slot = jnp.where(device < 0, device + ndev, device) * OWNED + (row & 3)
    hit = position_row[...] == slot
    cell = lax.broadcasted_iota(i32, (ndev * 8, blocks), 1).astype(f32)
    named = jnp.sum(jnp.where(hit, cell, 0.0), axis=1, keepdims=True).astype(i32)
    ids[...] = jnp.broadcast_to(named, (ndev * 8, 128))

    coarse = lax.broadcasted_iota(i32, (blocks, 128), 0)

    def look(i, seen):
        for n in range(8):
            seen = jnp.where(parent[pl.ds(i * 8 + n, 1), :] == coarse, 1.0, seen)
        return seen

    seen = lax.fori_loop(0, rows // 8, look, jnp.zeros((blocks, 128), f32))
    seen = jnp.broadcast_to(jnp.max(seen, axis=1, keepdims=True), (blocks, 128))
    below = (
        lax.broadcasted_iota(i32, (blocks, blocks), 1)
        < lax.broadcasted_iota(i32, (blocks, blocks), 0)
    )
    rank = jnp.dot(
        jnp.where(below, 1.0, 0.0).astype(bf16), seen.astype(bf16), preferred_element_type=f32
    )
    lanes = lax.broadcasted_iota(i32, (1, 128), 1)
    wanted = jnp.where(lanes < NAMED, lanes, jnp.where(lanes < 2 * NAMED, lanes - NAMED, -1))
    match = (rank == wanted.astype(f32)) & (seen > 0.0)
    list_row = jnp.sum(jnp.where(match, coarse.astype(f32) + 1.0, 0.0), axis=0, keepdims=True) - 1.0
    names_row[...] = jnp.broadcast_to(list_row, (8, 128)).astype(i32)
    names[...] = jnp.broadcast_to(list_row, (128, 128)).T[:NAMED].astype(i32)

    points = (lax.broadcasted_iota(i32, (ETA, 128), 0).astype(f32) + 0.5) / ETA
    log_a[...] = jnp.log(points)
    log_b[...] = jnp.log(1.0 - points)
    shape_sum = 1.0 / variance[...] - 1.0
    shape_a[...] = mean[...] * shape_sum - 1.0
    shape_b[...] = (1.0 - mean[...]) * shape_sum - 1.0
    grid[...] = thermal[...]

    spread = (
        (lax.broadcasted_iota(i32, (OWNED * SPEC, SPEC), 0) & (SPEC - 1))
        == lax.broadcasted_iota(i32, (OWNED * SPEC, SPEC), 1)
    ).astype(f32)
    for t in range(SPEC):
        columns[t] = jnp.broadcast_to(chem[:, t : t + 1], (SPEC, 128))

    weights = lax.dot_general(
        jnp.broadcast_to(weight[...], (8, SPEC)), spread, NT,
        precision=HIGHEST, preferred_element_type=f32,
    )
    mine = (lax.broadcasted_iota(i32, weights.shape, 0) & 3) == (
        lax.broadcasted_iota(i32, weights.shape, 1) >> 4
    )
    weights = jnp.where(mine, weights, 0.0)

    pl.semaphore_wait(barrier, ndev - 1)

    pending = []

    def hop(dz, dy, dx):
        def block(z, y, x):
            return state.at[
                core, lax.rem(x + xn, xn), lax.rem(z + zn, zn) * yn + lax.rem(y + yn, yn)
            ]

        if dy == 0 and dx == 0:
            there = (lax.rem(z + dz, zn) * yn + y, gy)
            here = block(z, y, x)
        else:
            there = (z * yn + lax.rem(y + dy, yn), lax.rem(x + dx, xn) * 2 + core)
            here = block(z - dz, y, x)
        come = block(z - dz, y - dy, x - dx)
        n = (dz * yn + dy) * xn + dx
        sems = (state_send.at[n], state_recv.at[n])
        return (
            pltpu.make_async_remote_copy(here, here, *sems, there, MESH),
            pltpu.make_async_remote_copy(come, come, *sems, there, MESH),
        )

    square = [(dy, dx) for dy in range(yn) for dx in range(xn) if dy or dx]

    def along_z(dz):
        return [hop(dz, 0, 0)]

    def over_square(dz):
        return [hop(dz, dy, dx) for dy, dx in square]

    def across():
        there = (gx, x * 2 + 1 - core)
        here = state.at[core]
        come = state.at[1 - core]
        sems = (state_send.at[0], state_recv.at[0])
        return [(
            pltpu.make_async_remote_copy(here, here, *sems, there, MESH),
            pltpu.make_async_remote_copy(come, come, *sems, there, MESH),
        )]

    def launch(copies):
        for out, _ in copies:
            out.start()
            pending.append(out)

    def arrive(copies):
        for _, come in copies:
            come.wait_recv()

    def halo(turn):
        low = (lax.rem(gx - 1 + gxn, gxn), gy)
        high = (lax.rem(gx + 1, gxn), gy)
        left = (gx, lax.rem(gy - 1 + gyn, gyn))
        right = (gx, lax.rem(gy + 1, gyn))
        source = grid if turn else thermal
        first = source.at[pl.ds(0, ys)]
        last = source.at[pl.ds((xs - 1) * ys, ys)]
        ends = [
            (last, face_x.at[turn, 0], high),
            (first, face_x.at[turn, 1], low),
            (own_y.at[turn], face_y.at[turn, 0], right),
            (own_y.at[turn], face_y.at[turn, 1], left),
        ]
        copies = [
            pltpu.make_async_remote_copy(
                s, d, halo_send.at[turn, n], halo_recv.at[turn, n], there, MESH
            )
            for n, (s, d, there) in enumerate(ends)
        ]
        return [(c, c) for c in copies]

    def send_halo(turn):
        now = grid[...]
        own_y[turn] = jnp.concatenate(
            [now[x * ys : x * ys + 1] for x in range(xs)]
            + [now[x * ys + ys - 1 : (x + 1) * ys] for x in range(xs)],
            axis=0,
        )
        launch(halo(turn))

    def exchange(source, target, turn, sign, send, recv):
        @pl.loop(1, ndev)
        def _(j):
            pltpu.make_async_remote_copy(
                source(j), target.at[turn, j], send.at[turn], recv.at[turn],
                place(me + sign * j), MESH,
            ).start()

        rest = target.at[turn, pl.ds(1, ndev - 1)]
        whole = pltpu.make_async_remote_copy(
            rest, rest, send.at[turn], recv.at[turn], place(me + 1), MESH
        )
        pending.append(whole)
        return whole

    half_row = lax.broadcasted_iota(i32, (8, 128), 0) < 4
    upper = (lax.broadcasted_iota(i32, (ndev * 8, 128), 0) & 4) == 0

    def split(values):
        high = values.astype(bf16)
        return [high, (values - high.astype(f32)).astype(bf16)]

    def same_cell():
        return ids[...] == names_row[0:1, :]

    def hits(r):
        return parent[pl.ds(r, 1), :] == names[...]

    def gather_row(r, first):
        hit = hits(r)
        here = mass[pl.ds(r, 1), :]
        parts = [jnp.where(hit, here * chi[pl.ds(r, 1), :], 0.0).astype(bf16)]
        if first:
            parts = [jnp.where(hit, here, 0.0).astype(bf16)] + parts
        return jnp.concatenate(parts, axis=0)

    def add_up(chosen, values):
        chosen = jnp.concatenate(chosen, axis=1)
        count = chosen.shape[0]
        total[128 - 32 - count : 96] += lax.dot_general(
            chosen, values, NT, preferred_element_type=f32
        )

    def first_turn(i, cells):
        chosen = []
        for n in range(ROWS):
            r = i * ROWS + n
            logits = shape_a[pl.ds(r, 1), :] * log_a[...] + shape_b[pl.ds(r, 1), :] * log_b[...]
            raised = jnp.exp(logits - jnp.max(logits, axis=0, keepdims=True))
            part = raised * (1.0 / jnp.sum(raised, axis=0, keepdims=True))
            table[i, :, n * 128 : (n + 1) * 128] = part
            table16[i, :, n * 128 : (n + 1) * 128] = part.astype(bf16)
            chosen.append(gather_row(r, True))
        add_up(chosen, table16[i])
        each = blocks // turns
        for n in range(each):
            c = i * each + n
            at = position[c]
            cells = tuple(
                jnp.where(at == me * OWNED + q, c, cells[q]) for q in range(OWNED)
            )
        return cells

    def second_turn(i, carry):
        add_up([gather_row(i * ROWS + n, False) for n in range(ROWS)], table16[i])
        return carry

    def reduce_sums(turn):
        lane_low = lax.broadcasted_iota(i32, (ndev * 8, 128), 1) < NAMED
        pick = jnp.where(same_cell() & (lane_low == upper), 1.0, 0.0).astype(bf16)
        sums = jnp.dot(
            jnp.concatenate([pick, pick], axis=1),
            jnp.concatenate(split(total[...]), axis=0),
            preferred_element_type=f32,
        )
        sent[turn] = sums.reshape(ndev, 8, 128)
        exchange(
            lambda j: sent.at[turn, j], got, turn, -1, sums_send, sums_recv
        ).wait_recv()
        return sent[turn, 0] + jnp.sum(got[turn, pl.ds(1, ndev - 1)], axis=0)

    def spread_rows(pieces):
        return jnp.concatenate(
            [jnp.broadcast_to(p, (SPEC, 128)) for p in pieces], axis=0
        )

    def block_of(slot):
        d = slot >> 2
        at = d & (gyn - 1)
        return state[at & 1, at >> 1, d // gyn, pl.ds((slot & 3) * SPEC, SPEC), :]

    def laplacian(current):
        edge = lax.broadcasted_iota(i32, current.shape, 1)
        left = jnp.where(edge == 0, current, pltpu.roll(current, 1, 1))
        right = jnp.where(edge == 127, current, pltpu.roll(current, 127, 1))
        return right - 2.0 * current + left

    def scalar_decay(turn, sums):
        if turn == 0:
            weights_known[...] = sums
        return (sums[4:8] + prior_flux) / (weights_known[0:4] + prior_weight)

    def advance(turn, cchi, cells):
        cchi = spread_rows([cchi[q : q + 1] for q in range(OWNED)])
        counts = jnp.concatenate(
            [jnp.full((SPEC, 128), increments[cells[q]] + 1, i32) for q in range(OWNED)], axis=0
        )
        fraction = 1.0 / counts.astype(f32)
        mixed = fraction * mixing_rate * cchi
        reacted = fraction * react_rate
        parts = []
        for q in range(OWNED):
            around = None
            for j in range(6):
                if turn == 0:
                    there = block_of(position[partners[j, cells[q]]])
                else:
                    n = (q * 6 + j) * SPEC
                    there = next_now[n : n + SPEC, :]
                around = there if around is None else around + there
            parts.append(around)
        around = jnp.concatenate(parts, axis=0)
        now = state0[...] if turn == 0 else species_out[...]
        now = now + coupling * (around - 6.0 * now)

        def substep(index, current):
            bent_rows[...] = jnp.tanh(current)
            sources = [None] * OWNED
            for t in range(SPEC):
                column = columns[t]
                for q in range(OWNED):
                    term = column * bent_rows[q * SPEC + t : q * SPEC + t + 1, :]
                    sources[q] = term if t == 0 else sources[q] + term
            source = jnp.concatenate(sources, axis=0)
            update = mixed * laplacian(current) + reacted * source
            return jnp.where(index < counts, current + update, current)

        now = lax.fori_loop(0, SUBMAX, substep, now)
        species_out[...] = now
        theta[turn, 0] = jnp.dot(weights, now, precision=HIGHEST, preferred_element_type=f32)

    def advance_near(cells):
        def prepare(j, carry):
            for q in range(OWNED):
                cell = partners[j, cells[q]]
                slot = position[cell]
                now = block_of(slot)
                around = None
                for k in range(6):
                    there = block_of(position[partners[k, cell]])
                    around = there if around is None else around + there
                d = me - (slot >> 2)
                d = jnp.where(d < 0, d + ndev, d)
                counts = jnp.full((SPEC, 128), increments[cell] + 1, i32)
                fraction = 1.0 / counts.astype(f32)
                rows_at = pl.ds((q * 6 + j) * SPEC, SPEC)
                next_now[rows_at, :] = now + coupling * (around - 6.0 * now)
                next_mixed[rows_at, :] = fraction * mixing_rate * known[0, d, pl.ds(slot & 3, 1), :]
                next_reacted[rows_at, :] = fraction * react_rate
                next_counts[rows_at, :] = counts
            return carry

        lax.fori_loop(0, 6, prepare, 0)
        high, low = split(chem[...])
        chem_wide = jnp.concatenate([high, high, low], axis=1)

        def substep(index, carry):
            current = next_now[...]
            high, low = split(jnp.tanh(current))

            def side(values):
                return jnp.concatenate(
                    [values[n * SPEC : (n + 1) * SPEC] for n in range(6 * OWNED)], axis=1
                )

            high, low = side(high), side(low)
            source = jnp.dot(
                chem_wide, jnp.concatenate([high, low, high], axis=0), preferred_element_type=f32
            )
            source = jnp.concatenate(
                [source[:, n * 128 : (n + 1) * 128] for n in range(6 * OWNED)], axis=0
            )
            update = next_mixed[...] * laplacian(current) + next_reacted[...] * source
            next_now[...] = jnp.where(index < next_counts[...], current + update, current)
            return carry

        lax.fori_loop(0, SUBMAX, substep, 0)

    def refine(turn):
        flat = theta[turn].reshape(ndev * 8, 128).T
        pick = jnp.where(same_cell() & upper, 1.0, 0.0).astype(bf16)
        whole = jnp.dot(
            jnp.concatenate(split(flat), axis=1),
            jnp.concatenate([pick, pick], axis=0),
            preferred_element_type=f32,
        )
        high = whole.astype(bf16).astype(f32)
        lanes_all = lax.broadcasted_iota(i32, (ETA, 128), 1)
        halves = jnp.where(lanes_all < NAMED, high, whole - high).astype(bf16)
        blank = jnp.zeros((128 - 2 * NAMED, 128), bf16)

        def body(i, carry):
            picks = []
            for n in range(ROWS):
                hit = jnp.where(hits(i * ROWS + n), 1.0, 0.0).astype(bf16)
                picks.append(jnp.concatenate([hit, hit, blank], axis=0))
            picked = jnp.dot(
                halves, jnp.concatenate(picks, axis=1), preferred_element_type=f32
            )
            value = jnp.sum(table[i] * picked, axis=0, keepdims=True)
            for n in range(ROWS):
                fine[pl.ds(i * ROWS + n, 1), :] = value[:, n * 128 : (n + 1) * 128]
            return carry

        lax.fori_loop(0, turns, body, 0)

    def diffuse(turn):
        arrive(halo(turn))
        now = grid[...]
        zero = jnp.zeros((ys, 128), f32)
        low_x = jnp.where(gx == 0, zero, face_x[turn, 0])
        high_x = jnp.where(gx == gxn - 1, zero, face_x[turn, 1])
        around = jnp.concatenate([now[ys:], high_x], axis=0)
        around = around + jnp.concatenate([low_x, now[:-ys]], axis=0)
        low_y = jnp.where(gy == 0, 0.0, face_y[turn, 0])
        high_y = jnp.where(gy == gyn - 1, 0.0, face_y[turn, 1])
        low_y = jnp.concatenate(
            [jnp.broadcast_to(low_y[xs + x : xs + x + 1], (ys, 128)) for x in range(xs)], axis=0
        )
        high_y = jnp.concatenate(
            [jnp.broadcast_to(high_y[x : x + 1], (ys, 128)) for x in range(xs)], axis=0
        )
        y = lax.rem(lax.broadcasted_iota(i32, (rows, 128), 0), ys)
        around = around + jnp.where(y == ys - 1, high_y, pltpu.roll(now, rows - 1, 0))
        around = around + jnp.where(y == 0, low_y, pltpu.roll(now, 1, 0))
        z = lax.broadcasted_iota(i32, (rows, 128), 1)
        around = around + jnp.where(z == 127, 0.0, pltpu.roll(now, 127, 1))
        around = around + jnp.where(z == 0, 0.0, pltpu.roll(now, 1, 1))
        return (
            now
            + thermal_diffusion * (around - 6.0 * now)
            + damping_contribution * (fine[...] - now)
        )

    def dissipate():
        chi[...] = decay[...] * (1.0 + 0.5 * jnp.tanh(grid[...]))

    state[core, x, gx] = state0[...]
    for dz in range(1, zn):
        launch(along_z(dz))
    launch(over_square(0))
    send_halo(0)
    dissipate()
    total[...] = jnp.zeros_like(total)
    cells = (jnp.int32(0),) * OWNED
    cells = lax.fori_loop(0, turns // 2, first_turn, cells)
    for dz in range(1, zn):
        arrive(along_z(dz))
        launch(over_square(dz))
    cells = lax.fori_loop(turns // 2, turns, first_turn, cells)
    sums = reduce_sums(0)
    cchi = scalar_decay(0, sums)
    known[0, 0] = jnp.concatenate([cchi, cchi], axis=0)
    for dz in range(zn):
        arrive(over_square(dz))
    launch(across())
    all_known = exchange(lambda j: known.at[0, 0], known, 0, 1, known_send, known_recv)
    arrive(across())
    advance(0, cchi, cells)
    moving = exchange(lambda j: theta.at[0, 0], theta, 0, 1, theta_send, theta_recv)
    all_known.wait_recv()
    advance_near(cells)
    moving.wait_recv()
    refine(0)
    grid[...] = diffuse(0)

    send_halo(1)
    dissipate()
    total[...] = jnp.zeros_like(total)
    lax.fori_loop(0, turns, second_turn, 0)
    sums = reduce_sums(1)
    advance(1, scalar_decay(1, sums), cells)
    exchange(lambda j: theta.at[1, 0], theta, 1, 1, theta_send, theta_recv).wait_recv()
    refine(1)
    thermal_out[...] = diffuse(1)

    for copy in pending:
        copy.wait_send()


def shards(
    thermal_grid,
    average_blend_fraction,
    normalized_blend_variance,
    small_volume_mass,
    bare_scalar_decay,
    parent_block,
    species_given_block,
    block_position,
    face_partners,
    reaction_increments,
    chemical_coupling,
    species_thermal_weight,
):
    gxn, gyn = lax.axis_size("gx"), lax.axis_size("gy")
    ndev = gxn * gyn
    blocks = block_position.shape[0]
    xs, ys, zs = thermal_grid.shape
    rows = xs * ys
    turns = rows // ROWS
    assert blocks == ndev * OWNED and zs == 128 and rows % (2 * ROWS) == 0
    vmem = pl.BlockSpec(memory_space=pltpu.VMEM)
    dma = pltpu.SemaphoreType.DMA
    species, thermal = pl.pallas_call(
        functools.partial(kernel, gxn, gyn, xs, ys),
        out_shape=(
            jax.ShapeDtypeStruct((OWNED * SPEC, ETA), f32),
            jax.ShapeDtypeStruct((rows, zs), f32),
        ),
        in_specs=[pl.BlockSpec(memory_space=pltpu.HBM)] * 13,
        out_specs=(vmem, vmem),
        scratch_shapes=[
            *[pltpu.VMEM((rows, zs), f32)] * 5,
            pltpu.VMEM((rows, zs), i32),
            pltpu.VMEM((OWNED * SPEC, ETA), f32),
            pltpu.VMEM((1, blocks), i32),
            pltpu.VMEM((SPEC, SPEC), f32),
            pltpu.VMEM((1, SPEC), f32),
            pltpu.SMEM((blocks,), i32),
            pltpu.SMEM((6, blocks), i32),
            pltpu.SMEM((blocks,), i32),
            dma((13,)),
            pltpu.VMEM((ndev * 8, 128), i32),
            pltpu.VMEM((NAMED, 128), i32),
            pltpu.VMEM((8, 128), i32),
            pltpu.VMEM((OWNED * SPEC, ETA), f32),
            pltpu.VMEM((SPEC, SPEC, ETA), f32),
            pltpu.VMEM((8, ETA), f32),
            pltpu.VMEM((ETA, 128), f32),
            pltpu.VMEM((ETA, 128), f32),
            pltpu.VMEM((rows, zs), f32),
            pltpu.VMEM((rows, zs), f32),
            pltpu.VMEM((rows, zs), f32),
            pltpu.VMEM((rows, zs), f32),
            pltpu.VMEM((rows, zs), f32),
            pltpu.VMEM((turns, ETA, ROWS * 128), f32),
            pltpu.VMEM((turns, ETA, ROWS * 128), bf16),
            pltpu.VMEM((128, ETA), f32),
            pltpu.VMEM((1, ndev, 8, ETA), f32),
            *[pltpu.VMEM((6 * OWNED * SPEC, ETA), f32)] * 3,
            pltpu.VMEM((6 * OWNED * SPEC, ETA), i32),
            pltpu.VMEM((STEPS, ndev, 8, ETA), f32),
            pltpu.VMEM((STEPS, ndev, 8, ETA), f32),
            pltpu.VMEM((STEPS, ndev, 8, ETA), f32),
            pltpu.VMEM((2, gyn // 2, gxn, OWNED * SPEC, ETA), f32),
            pltpu.VMEM((STEPS, 2, ys, zs), f32),
            pltpu.VMEM((STEPS, 2, 2 * xs, zs), f32),
            pltpu.VMEM((STEPS, 2 * xs, zs), f32),
            dma((STEPS,)),
            dma((STEPS,)),
            dma((1,)),
            dma((1,)),
            dma((STEPS,)),
            dma((STEPS,)),
            dma((ndev // 2,)),
            dma((ndev // 2,)),
            dma((STEPS, 4)),
            dma((STEPS, 4)),
        ],
        compiler_params=pltpu.CompilerParams(
            collective_id=0, has_side_effects=True, vmem_limit_bytes=63 * 1024 * 1024
        ),
    )(
        thermal_grid.reshape(rows, zs),
        average_blend_fraction.reshape(rows, zs),
        normalized_blend_variance.reshape(rows, zs),
        small_volume_mass.reshape(rows, zs),
        bare_scalar_decay.reshape(rows, zs),
        parent_block.reshape(rows, zs),
        species_given_block.reshape(OWNED * SPEC, ETA),
        block_position.reshape(1, blocks),
        chemical_coupling,
        species_thermal_weight.reshape(1, SPEC),
        block_position,
        face_partners.T,
        reaction_increments,
    )
    return (species.reshape(OWNED, SPEC, ETA), thermal.reshape(xs, ys, zs))


def solution(mesh):
    fine = P("gx", "gy", None)
    return jax.shard_map(
        shards,
        mesh=mesh,
        in_specs=(fine,) * 6 + (P(("gx", "gy"), None, None),) + (P(),) * 5,
        out_specs=(P(("gx", "gy"), None, None), fine),
        check_vma=False,
    )
```

```python
import functools

import jax
import jax.numpy as jnp
from jax import lax
from jax.experimental import pallas as pl
from jax.experimental.pallas import tpu as pltpu
from jax.sharding import PartitionSpec as P

ETA = 128
SPEC = 16
SUBMAX = 16
STEPS = 2
ROWS = 8
OWNED = 4
NAMED = 48

coupling = 0.05
mixing_rate = 0.2
react_rate = 0.5
prior_weight = 1.0
prior_flux = 0.5
thermal_diffusion = 0.1
damping_contribution = 0.3

MESH = pl.DeviceIdType.MESH
HIGHEST = lax.Precision.HIGHEST
NT = (((1,), (1,)), ((), ()))
f32, bf16, i32 = jnp.float32, jnp.bfloat16, jnp.int32


def kernel(
    gxn, gyn, xs, ys,
    thermal_in, mean_in, variance_in, mass_in, decay_in, parent_in, state0_in, position_row_in,
    chem_in, weight_in, position_in, partners_in, increments_in,
    species_out, thermal_out,
    thermal, mean, variance, mass, decay, parent, state0, position_row, chem, weight,
    position, partners, increments, load,
    ids, names, names_row, bent_rows, columns, weights_known, weights_of, ids_short, log_a, log_b, shape_a, shape_b, chi, grid, fine, table, table16, total,
    known, next_now, next_mixed, next_reacted, next_counts,
    sent, got, sent_short, got_short, theta, state, face_x, face_y, own_y,
    sums_send, sums_recv, short_send, short_recv, known_send, known_recv, theta_send, theta_recv, state_send, state_recv, halo_send, halo_recv,
):
    ndev = gxn * gyn
    blocks = ndev * OWNED
    rows = xs * ys
    turns = rows // ROWS
    unroll = ndev - 1 if ndev <= 32 else 1
    xn = gyn // 2
    yn = xn if gxn % xn == 0 else 1
    zn = gxn // yn
    gx, gy = lax.axis_index("gx"), lax.axis_index("gy")
    me = gx * gyn + gy
    core, x = gy & 1, gy >> 1
    y, z = lax.rem(gx, yn), gx // yn

    def place(device):
        device = (device + ndev) & (ndev - 1)
        return (device >> (gyn.bit_length() - 1), device & (gyn - 1))

    barrier = pltpu.get_barrier_semaphore()

    @pl.loop(1, ndev, unroll=unroll)
    def _(j):
        pl.semaphore_signal(barrier, inc=1, device_id=place(me + j), device_id_type=MESH)

    loads = [
        pltpu.make_async_copy(source, target, load.at[n])
        for n, (source, target) in enumerate((
            (state0_in, state0), (thermal_in, thermal), (position_row_in, position_row),
            (parent_in, parent), (variance_in, variance), (mean_in, mean), (mass_in, mass),
            (decay_in, decay), (chem_in, chem), (weight_in, weight),
            (position_in, position), (partners_in, partners), (increments_in, increments),
        ))
    ]
    for copy in loads:
        copy.start()
    loads[0].wait()
    pl.semaphore_wait(barrier, ndev - 1)

    def prepare_all():
        for copy in loads[2:]:
            copy.wait()
        def cells_of(count, shift):
            row = lax.broadcasted_iota(i32, (count, blocks), 0)
            device = me - (row >> shift)
            slot = jnp.where(device < 0, device + ndev, device) * OWNED + (row & 3)
            cell = lax.broadcasted_iota(i32, (count, blocks), 1).astype(f32)
            found = jnp.where(position_row[...] == slot, cell, 0.0)
            named = jnp.sum(found, axis=1, keepdims=True).astype(i32)
            return jnp.broadcast_to(named, (count, 128))

        ids[...] = cells_of(ndev * 8, 3)
        ids_short[...] = cells_of(ndev * 4, 2)

        coarse = lax.broadcasted_iota(i32, (blocks, 128), 0)

        def look(i, seen):
            for n in range(8):
                seen = jnp.where(parent[pl.ds(i * 8 + n, 1), :] == coarse, 1.0, seen)
            return seen

        seen = lax.fori_loop(0, rows // 8, look, jnp.zeros((blocks, 128), f32))
        seen = jnp.broadcast_to(jnp.max(seen, axis=1, keepdims=True), (blocks, 128))
        below = (
            lax.broadcasted_iota(i32, (blocks, blocks), 1)
            < lax.broadcasted_iota(i32, (blocks, blocks), 0)
        )
        rank = jnp.dot(
            jnp.where(below, 1.0, 0.0).astype(bf16), seen.astype(bf16), preferred_element_type=f32
        )
        lanes = lax.broadcasted_iota(i32, (1, 128), 1)
        wanted = jnp.where(lanes < NAMED, lanes, jnp.where(lanes < 2 * NAMED, lanes - NAMED, -1))
        match = (rank == wanted.astype(f32)) & (seen > 0.0)
        list_row = jnp.sum(jnp.where(match, coarse.astype(f32) + 1.0, 0.0), axis=0, keepdims=True) - 1.0
        names_row[...] = jnp.broadcast_to(list_row, (8, 128)).astype(i32)
        names[...] = jnp.broadcast_to(list_row, (128, 128)).T[:NAMED].astype(i32)

        points = (lax.broadcasted_iota(i32, (ETA, 128), 0).astype(f32) + 0.5) / ETA
        log_a[...] = jnp.log(points)
        log_b[...] = jnp.log(1.0 - points)
        shape_sum = 1.0 / variance[...] - 1.0
        shape_a[...] = mean[...] * shape_sum - 1.0
        shape_b[...] = (1.0 - mean[...]) * shape_sum - 1.0

        for t in range(SPEC):
            columns[t] = jnp.broadcast_to(chem[:, t : t + 1], (SPEC, 128))

        spread = (
            (lax.broadcasted_iota(i32, (OWNED * SPEC, SPEC), 0) & (SPEC - 1))
            == lax.broadcasted_iota(i32, (OWNED * SPEC, SPEC), 1)
        ).astype(f32)
        weights = lax.dot_general(
            jnp.broadcast_to(weight[...], (OWNED, SPEC)), spread, NT,
            precision=HIGHEST, preferred_element_type=f32,
        )
        mine = lax.broadcasted_iota(i32, weights.shape, 0) == (
            lax.broadcasted_iota(i32, weights.shape, 1) >> 4
        )
        weights = jnp.where(mine, weights, 0.0)
        weights_of[...] = weights

    pending = []

    def hop(dz, dy, dx):
        def block(z, y, x):
            return state.at[
                core, lax.rem(x + xn, xn), lax.rem(z + zn, zn) * yn + lax.rem(y + yn, yn)
            ]

        if dy == 0 and dx == 0:
            there = (lax.rem(z + dz, zn) * yn + y, gy)
            here = block(z, y, x)
        else:
            there = (z * yn + lax.rem(y + dy, yn), lax.rem(x + dx, xn) * 2 + core)
            here = block(z - dz, y, x)
        come = block(z - dz, y - dy, x - dx)
        n = (dz * yn + dy) * xn + dx
        sems = (state_send.at[n], state_recv.at[n])
        return (
            pltpu.make_async_remote_copy(here, here, *sems, there, MESH),
            pltpu.make_async_remote_copy(come, come, *sems, there, MESH),
        )

    square = [(dy, dx) for dy in range(yn) for dx in range(xn) if dy or dx]

    def along_z(dz):
        return [hop(dz, 0, 0)]

    def over_square(dz):
        return [hop(dz, dy, dx) for dy, dx in square]

    def across():
        there = (gx, x * 2 + 1 - core)
        here = state.at[core]
        come = state.at[1 - core]
        sems = (state_send.at[0], state_recv.at[0])
        return [(
            pltpu.make_async_remote_copy(here, here, *sems, there, MESH),
            pltpu.make_async_remote_copy(come, come, *sems, there, MESH),
        )]

    def launch(copies):
        for out, _ in copies:
            out.start()
            pending.append(out)

    def arrive(copies):
        for _, come in copies:
            come.wait_recv()

    def halo(turn):
        low = (lax.rem(gx - 1 + gxn, gxn), gy)
        high = (lax.rem(gx + 1, gxn), gy)
        left = (gx, lax.rem(gy - 1 + gyn, gyn))
        right = (gx, lax.rem(gy + 1, gyn))
        source = grid if turn else thermal
        first = source.at[pl.ds(0, ys)]
        last = source.at[pl.ds((xs - 1) * ys, ys)]
        ends = [
            (last, face_x.at[turn, 0], high),
            (first, face_x.at[turn, 1], low),
            (own_y.at[turn], face_y.at[turn, 0], right),
            (own_y.at[turn], face_y.at[turn, 1], left),
        ]
        copies = [
            pltpu.make_async_remote_copy(
                s, d, halo_send.at[turn, n], halo_recv.at[turn, n], there, MESH
            )
            for n, (s, d, there) in enumerate(ends)
        ]
        return [(c, c) for c in copies]

    def send_halo(turn):
        now = grid[...]
        own_y[turn] = jnp.concatenate(
            [now[x * ys : x * ys + 1] for x in range(xs)]
            + [now[x * ys + ys - 1 : (x + 1) * ys] for x in range(xs)],
            axis=0,
        )
        launch(halo(turn))

    def exchange(source, target, turn, sign, send, recv):
        @pl.loop(1, ndev, unroll=unroll)
        def _(j):
            pltpu.make_async_remote_copy(
                source(j), target.at[turn, j], send.at[turn], recv.at[turn],
                place(me + sign * j), MESH,
            ).start()

        rest = target.at[turn, pl.ds(1, ndev - 1)]
        whole = pltpu.make_async_remote_copy(
            rest, rest, send.at[turn], recv.at[turn], place(me + 1), MESH
        )
        pending.append(whole)
        return whole

    half_row = lax.broadcasted_iota(i32, (8, 128), 0) < 4
    upper = (lax.broadcasted_iota(i32, (ndev * 8, 128), 0) & 4) == 0

    def split(values):
        high = values.astype(bf16)
        return [high, (values - high.astype(f32)).astype(bf16)]

    def hits(r):
        return parent[pl.ds(r, 1), :] == names[...]

    def gather_row(r, first):
        hit = hits(r)
        here = mass[pl.ds(r, 1), :]
        parts = [jnp.where(hit, here * chi[pl.ds(r, 1), :], 0.0).astype(bf16)]
        if first:
            parts = [jnp.where(hit, here, 0.0).astype(bf16)] + parts
        return jnp.concatenate(parts, axis=0)

    def add_up(chosen, values):
        chosen = jnp.concatenate(chosen, axis=1)
        count = chosen.shape[0]
        total[128 - 32 - count : 96] += lax.dot_general(
            chosen, values, NT, preferred_element_type=f32
        )

    def first_turn(i, cells):
        chosen = []
        for n in range(ROWS):
            r = i * ROWS + n
            logits = shape_a[pl.ds(r, 1), :] * log_a[...] + shape_b[pl.ds(r, 1), :] * log_b[...]
            raised = jnp.exp(logits - jnp.max(logits, axis=0, keepdims=True))
            part = raised * (1.0 / jnp.sum(raised, axis=0, keepdims=True))
            table[i, :, n * 128 : (n + 1) * 128] = part
            table16[i, :, n * 128 : (n + 1) * 128] = part.astype(bf16)
            chosen.append(gather_row(r, True))
        add_up(chosen, table16[i])
        each = blocks // turns
        for n in range(each):
            c = i * each + n
            at = position[c]
            cells = tuple(
                jnp.where(at == me * OWNED + q, c, cells[q]) for q in range(OWNED)
            )
        return cells

    def second_turn(i, carry):
        add_up([gather_row(i * ROWS + n, False) for n in range(ROWS)], table16[i])
        return carry

    def pick_sums(pick):
        pick = jnp.where(pick, 1.0, 0.0).astype(bf16)
        return jnp.dot(
            jnp.concatenate([pick, pick], axis=1),
            jnp.concatenate(split(total[...]), axis=0),
            preferred_element_type=f32,
        )

    def send_sums(turn):
        if turn == 0:
            low = lax.broadcasted_iota(i32, (ndev * 8, 128), 1) < NAMED
            sums = pick_sums((ids[...] == names_row[0:1, :]) & (low == upper))
            sent[0] = sums.reshape(ndev, 8, 128)
            return exchange(lambda j: sent.at[0, j], got, 0, -1, sums_send, sums_recv)
        low = lax.broadcasted_iota(i32, (ndev * 4, 128), 1) < NAMED
        sums = pick_sums((ids_short[...] == names_row[0:1, :]) & ~low)
        sent_short[0] = sums.reshape(ndev, 4, 128)
        return exchange(
            lambda j: sent_short.at[0, j], got_short, 0, -1, short_send, short_recv
        )

    def scalar_decay(turn):
        if turn == 0:
            sums = sent[0, 0] + jnp.sum(got[0, pl.ds(1, ndev - 1)], axis=0)
            weights_known[...] = sums[0:4]
            flux = sums[4:8]
        else:
            flux = sent_short[0, 0] + jnp.sum(got_short[0, pl.ds(1, ndev - 1)], axis=0)
        return (flux + prior_flux) / (weights_known[...] + prior_weight)

    def spread_rows(pieces):
        return jnp.concatenate(
            [jnp.broadcast_to(p, (SPEC, 128)) for p in pieces], axis=0
        )

    def block_of(slot):
        d = slot >> 2
        at = d & (gyn - 1)
        return state[at & 1, at >> 1, d >> (gyn.bit_length() - 1), pl.ds((slot & 3) * SPEC, SPEC), :]

    def laplacian(current):
        edge = lax.broadcasted_iota(i32, current.shape, 1)
        left = jnp.where(edge == 0, current, pltpu.roll(current, 1, 1))
        right = jnp.where(edge == 127, current, pltpu.roll(current, 127, 1))
        return right - 2.0 * current + left

    def advance(turn, cchi, cells):
        cchi = spread_rows([cchi[q : q + 1] for q in range(OWNED)])
        counts = jnp.concatenate(
            [jnp.full((SPEC, 128), increments[cells[q]] + 1, i32) for q in range(OWNED)], axis=0
        )
        fraction = 1.0 / counts.astype(f32)
        mixed = fraction * mixing_rate * cchi
        reacted = fraction * react_rate
        parts = []
        for q in range(OWNED):
            around = None
            for j in range(6):
                if turn == 0:
                    there = block_of(position[partners[j, cells[q]]])
                else:
                    n = (q * 6 + j) * SPEC
                    there = next_now[n : n + SPEC, :]
                around = there if around is None else around + there
            parts.append(around)
        around = jnp.concatenate(parts, axis=0)
        now = state0[...] if turn == 0 else species_out[...]
        now = now + coupling * (around - 6.0 * now)

        def substep(index, current):
            bent_rows[...] = jnp.tanh(current)
            sources = [None] * OWNED
            for t in range(SPEC):
                column = columns[t]
                for q in range(OWNED):
                    term = column * bent_rows[q * SPEC + t : q * SPEC + t + 1, :]
                    sources[q] = term if t == 0 else sources[q] + term
            source = jnp.concatenate(sources, axis=0)
            update = mixed * laplacian(current) + reacted * source
            return jnp.where(index < counts, current + update, current)

        now = lax.fori_loop(0, SUBMAX, substep, now)
        species_out[...] = now
        theta[turn, 0] = jnp.dot(weights_of[...], now, precision=HIGHEST, preferred_element_type=f32)

    def advance_near(cells):
        def prepare(j, carry):
            for q in range(OWNED):
                cell = partners[j, cells[q]]
                slot = position[cell]
                now = block_of(slot)
                around = None
                for k in range(6):
                    there = block_of(position[partners[k, cell]])
                    around = there if around is None else around + there
                d = me - (slot >> 2)
                d = jnp.where(d < 0, d + ndev, d)
                counts = jnp.full((SPEC, 128), increments[cell] + 1, i32)
                fraction = 1.0 / counts.astype(f32)
                rows_at = pl.ds((q * 6 + j) * SPEC, SPEC)
                next_now[rows_at, :] = now + coupling * (around - 6.0 * now)
                next_mixed[rows_at, :] = fraction * mixing_rate * known[0, d, pl.ds(slot & 3, 1), :]
                next_reacted[rows_at, :] = fraction * react_rate
                next_counts[rows_at, :] = counts
            return carry

        lax.fori_loop(0, 6, prepare, 0)

    def substeps_near(first, last):
        high, low = split(chem[...])
        chem_wide = jnp.concatenate([high, high, low], axis=1)

        def substep(index, carry):
            current = next_now[...]
            high, low = split(jnp.tanh(current))

            def side(values):
                return jnp.concatenate(
                    [values[n * SPEC : (n + 1) * SPEC] for n in range(6 * OWNED)], axis=1
                )

            high, low = side(high), side(low)
            source = jnp.dot(
                chem_wide, jnp.concatenate([high, low, high], axis=0), preferred_element_type=f32
            )
            source = jnp.concatenate(
                [source[:, n * 128 : (n + 1) * 128] for n in range(6 * OWNED)], axis=0
            )
            update = next_mixed[...] * laplacian(current) + next_reacted[...] * source
            next_now[...] = jnp.where(index < next_counts[...], current + update, current)
            return carry

        lax.fori_loop(first, last, substep, 0)

    def refine(turn):
        flat = theta[turn].reshape(ndev * 4, 128).T
        pick = jnp.where(ids_short[...] == names_row[0:1, :], 1.0, 0.0).astype(bf16)
        whole = jnp.dot(
            jnp.concatenate(split(flat), axis=1),
            jnp.concatenate([pick, pick], axis=0),
            preferred_element_type=f32,
        )
        high = whole.astype(bf16).astype(f32)
        lanes_all = lax.broadcasted_iota(i32, (ETA, 128), 1)
        halves = jnp.where(lanes_all < NAMED, high, whole - high).astype(bf16)
        blank = jnp.zeros((128 - 2 * NAMED, 128), bf16)

        def body(i, carry):
            picks = []
            for n in range(ROWS):
                hit = jnp.where(hits(i * ROWS + n), 1.0, 0.0).astype(bf16)
                picks.append(jnp.concatenate([hit, hit, blank], axis=0))
            picked = jnp.dot(
                halves, jnp.concatenate(picks, axis=1), preferred_element_type=f32
            )
            value = jnp.sum(table[i] * picked, axis=0, keepdims=True)
            for n in range(ROWS):
                fine[pl.ds(i * ROWS + n, 1), :] = value[:, n * 128 : (n + 1) * 128]
            return carry

        lax.fori_loop(0, turns, body, 0)

    def diffuse(turn):
        arrive(halo(turn))
        now = grid[...]
        zero = jnp.zeros((ys, 128), f32)
        low_x = jnp.where(gx == 0, zero, face_x[turn, 0])
        high_x = jnp.where(gx == gxn - 1, zero, face_x[turn, 1])
        around = jnp.concatenate([now[ys:], high_x], axis=0)
        around = around + jnp.concatenate([low_x, now[:-ys]], axis=0)
        low_y = jnp.where(gy == 0, 0.0, face_y[turn, 0])
        high_y = jnp.where(gy == gyn - 1, 0.0, face_y[turn, 1])
        low_y = jnp.concatenate(
            [jnp.broadcast_to(low_y[xs + x : xs + x + 1], (ys, 128)) for x in range(xs)], axis=0
        )
        high_y = jnp.concatenate(
            [jnp.broadcast_to(high_y[x : x + 1], (ys, 128)) for x in range(xs)], axis=0
        )
        y = lax.rem(lax.broadcasted_iota(i32, (rows, 128), 0), ys)
        around = around + jnp.where(y == ys - 1, high_y, pltpu.roll(now, rows - 1, 0))
        around = around + jnp.where(y == 0, low_y, pltpu.roll(now, 1, 0))
        z = lax.broadcasted_iota(i32, (rows, 128), 1)
        around = around + jnp.where(z == 127, 0.0, pltpu.roll(now, 127, 1))
        around = around + jnp.where(z == 0, 0.0, pltpu.roll(now, 1, 1))
        return (
            now
            + thermal_diffusion * (around - 6.0 * now)
            + damping_contribution * (fine[...] - now)
        )

    def dissipate():
        chi[...] = decay[...] * (1.0 + 0.5 * jnp.tanh(grid[...]))

    state[core, x, gx] = state0[...]
    for dz in range(1, zn):
        launch(along_z(dz))
    launch(over_square(0))
    loads[1].wait()
    grid[...] = thermal[...]
    send_halo(0)
    prepare_all()
    dissipate()
    total[...] = jnp.zeros_like(total)
    cells = (jnp.int32(0),) * OWNED
    cells = lax.fori_loop(0, turns // 2, first_turn, cells)
    for dz in range(1, zn):
        arrive(along_z(dz))
        launch(over_square(dz))
    cells = lax.fori_loop(turns // 2, turns, first_turn, cells)
    send_sums(0).wait_recv()
    cchi = scalar_decay(0)
    known[0, 0] = cchi
    for dz in range(zn):
        arrive(over_square(dz))
    launch(across())
    all_known = exchange(lambda j: known.at[0, 0], known, 0, 1, known_send, known_recv)
    arrive(across())
    advance(0, cchi, cells)
    moving = exchange(lambda j: theta.at[0, 0], theta, 0, 1, theta_send, theta_recv)
    all_known.wait_recv()
    advance_near(cells)
    substeps_near(0, SUBMAX // 2)
    moving.wait_recv()
    refine(0)
    grid[...] = diffuse(0)

    send_halo(1)
    dissipate()
    total[...] = jnp.zeros_like(total)
    lax.fori_loop(0, turns, second_turn, 0)
    moving = send_sums(1)
    substeps_near(SUBMAX // 2, SUBMAX)
    moving.wait_recv()
    advance(1, scalar_decay(1), cells)
    exchange(lambda j: theta.at[1, 0], theta, 1, 1, theta_send, theta_recv).wait_recv()
    refine(1)
    thermal_out[...] = diffuse(1)

    for copy in pending:
        copy.wait_send()


def shards(
    thermal_grid,
    average_blend_fraction,
    normalized_blend_variance,
    small_volume_mass,
    bare_scalar_decay,
    parent_block,
    species_given_block,
    block_position,
    face_partners,
    reaction_increments,
    chemical_coupling,
    species_thermal_weight,
):
    gxn, gyn = lax.axis_size("gx"), lax.axis_size("gy")
    ndev = gxn * gyn
    blocks = block_position.shape[0]
    xs, ys, zs = thermal_grid.shape
    rows = xs * ys
    turns = rows // ROWS
    assert ndev & (ndev - 1) == 0 and gyn & (gyn - 1) == 0
    assert blocks == ndev * OWNED and zs == 128 and rows % (2 * ROWS) == 0
    vmem = pl.BlockSpec(memory_space=pltpu.VMEM)
    dma = pltpu.SemaphoreType.DMA
    species, thermal = pl.pallas_call(
        functools.partial(kernel, gxn, gyn, xs, ys),
        out_shape=(
            jax.ShapeDtypeStruct((OWNED * SPEC, ETA), f32),
            jax.ShapeDtypeStruct((rows, zs), f32),
        ),
        in_specs=[pl.BlockSpec(memory_space=pltpu.HBM)] * 13,
        out_specs=(vmem, vmem),
        scratch_shapes=[
            *[pltpu.VMEM((rows, zs), f32)] * 5,
            pltpu.VMEM((rows, zs), i32),
            pltpu.VMEM((OWNED * SPEC, ETA), f32),
            pltpu.VMEM((1, blocks), i32),
            pltpu.VMEM((SPEC, SPEC), f32),
            pltpu.VMEM((1, SPEC), f32),
            pltpu.SMEM((blocks,), i32),
            pltpu.SMEM((6, blocks), i32),
            pltpu.SMEM((blocks,), i32),
            dma((13,)),
            pltpu.VMEM((ndev * 8, 128), i32),
            pltpu.VMEM((NAMED, 128), i32),
            pltpu.VMEM((8, 128), i32),
            pltpu.VMEM((OWNED * SPEC, ETA), f32),
            pltpu.VMEM((SPEC, SPEC, ETA), f32),
            pltpu.VMEM((4, ETA), f32),
            pltpu.VMEM((OWNED, OWNED * SPEC), f32),
            pltpu.VMEM((ndev * 4, 128), i32),
            pltpu.VMEM((ETA, 128), f32),
            pltpu.VMEM((ETA, 128), f32),
            pltpu.VMEM((rows, zs), f32),
            pltpu.VMEM((rows, zs), f32),
            pltpu.VMEM((rows, zs), f32),
            pltpu.VMEM((rows, zs), f32),
            pltpu.VMEM((rows, zs), f32),
            pltpu.VMEM((turns, ETA, ROWS * 128), f32),
            pltpu.VMEM((turns, ETA, ROWS * 128), bf16),
            pltpu.VMEM((128, ETA), f32),
            pltpu.VMEM((1, ndev, 4, ETA), f32),
            *[pltpu.VMEM((6 * OWNED * SPEC, ETA), f32)] * 3,
            pltpu.VMEM((6 * OWNED * SPEC, ETA), i32),
            pltpu.VMEM((1, ndev, 8, ETA), f32),
            pltpu.VMEM((1, ndev, 8, ETA), f32),
            pltpu.VMEM((1, ndev, 4, ETA), f32),
            pltpu.VMEM((1, ndev, 4, ETA), f32),
            pltpu.VMEM((STEPS, ndev, 4, ETA), f32),
            pltpu.VMEM((2, gyn // 2, gxn, OWNED * SPEC, ETA), f32),
            pltpu.VMEM((STEPS, 2, ys, zs), f32),
            pltpu.VMEM((STEPS, 2, 2 * xs, zs), f32),
            pltpu.VMEM((STEPS, 2 * xs, zs), f32),
            dma((1,)),
            dma((1,)),
            dma((1,)),
            dma((1,)),
            dma((1,)),
            dma((1,)),
            dma((STEPS,)),
            dma((STEPS,)),
            dma((ndev // 2,)),
            dma((ndev // 2,)),
            dma((STEPS, 4)),
            dma((STEPS, 4)),
        ],
        compiler_params=pltpu.CompilerParams(
            collective_id=0, has_side_effects=True, vmem_limit_bytes=63 * 1024 * 1024
        ),
    )(
        thermal_grid.reshape(rows, zs),
        average_blend_fraction.reshape(rows, zs),
        normalized_blend_variance.reshape(rows, zs),
        small_volume_mass.reshape(rows, zs),
        bare_scalar_decay.reshape(rows, zs),
        parent_block.reshape(rows, zs),
        species_given_block.reshape(OWNED * SPEC, ETA),
        block_position.reshape(1, blocks),
        chemical_coupling,
        species_thermal_weight.reshape(1, SPEC),
        block_position,
        face_partners.T,
        reaction_increments,
    )
    return (species.reshape(OWNED, SPEC, ETA), thermal.reshape(xs, ys, zs))


def solution(mesh):
    fine = P("gx", "gy", None)
    return jax.shard_map(
        shards,
        mesh=mesh,
        in_specs=(fine,) * 6 + (P(("gx", "gy"), None, None),) + (P(),) * 5,
        out_specs=(P(("gx", "gy"), None, None), fine),
        check_vma=False,
    )
```

```python
import functools

import jax
import jax.numpy as jnp
from jax import lax
from jax.experimental import pallas as pl
from jax.experimental.pallas import tpu as pltpu
from jax.sharding import PartitionSpec as P

ETA = 128
SPEC = 16
SUBMAX = 16
STEPS = 2
ROWS = 16
OWNED = 4
NAMED = 48

coupling = 0.05
mixing_rate = 0.2
react_rate = 0.5
prior_weight = 1.0
prior_flux = 0.5
thermal_diffusion = 0.1
damping_contribution = 0.3

MESH = pl.DeviceIdType.MESH
HIGHEST = lax.Precision.HIGHEST
NT = (((1,), (1,)), ((), ()))
f32, bf16, i32 = jnp.float32, jnp.bfloat16, jnp.int32


def kernel(
    gxn, gyn, xs, ys,
    thermal_in, mean_in, variance_in, mass_in, decay_in, parent_in, state0_in, position_row_in,
    chem_in, weight_in, position_in, partners_in, increments_in,
    result,
    thermal, mean, variance, mass, decay, parent, state0, position_row, chem, weight,
    position, partners, increments, load,
    ids, names, names_row, bent_rows, columns, weights_known, weights_of, ids_short, log_a, log_b, shape_a, shape_b, chi, grid, fine, table, table16, total,
    known, next_now, next_mixed, next_reacted, next_counts,
    sent, got, sent_short, got_short, theta, state, face_x, face_y, own_y,
    sums_send, sums_recv, short_send, short_recv, known_send, known_recv, theta_send, theta_recv, state_send, state_recv, halo_send, halo_recv,
):
    ndev = gxn * gyn
    blocks = ndev * OWNED
    rows = xs * ys
    turns = rows // ROWS
    unroll = ndev - 1 if ndev <= 32 else 1
    xn = gyn // 2
    yn = xn if gxn % xn == 0 else 1
    zn = gxn // yn
    gx, gy = lax.axis_index("gx"), lax.axis_index("gy")
    me = gx * gyn + gy
    core, x = gy & 1, gy >> 1
    y, z = lax.rem(gx, yn), gx // yn

    def place(device):
        device = (device + ndev) & (ndev - 1)
        return (device >> (gyn.bit_length() - 1), device & (gyn - 1))

    barrier = pltpu.get_barrier_semaphore()

    @pl.loop(1, ndev, unroll=unroll)
    def _(j):
        pl.semaphore_signal(barrier, inc=1, device_id=place(me + j), device_id_type=MESH)

    loads = [
        pltpu.make_async_copy(source, target, load.at[n])
        for n, (source, target) in enumerate((
            (state0_in, state0), (thermal_in, thermal), (position_row_in, position_row),
            (parent_in, parent), (variance_in, variance), (mean_in, mean), (mass_in, mass),
            (decay_in, decay), (chem_in, chem), (weight_in, weight),
            (position_in, position), (partners_in, partners), (increments_in, increments),
        ))
    ]
    for copy in loads:
        copy.start()
    loads[0].wait()
    pl.semaphore_wait(barrier, ndev - 1)

    def prepare_all():
        for copy in loads[2:]:
            copy.wait()
        def cells_of(count, shift):
            row = lax.broadcasted_iota(i32, (count, blocks), 0)
            device = me - (row >> shift)
            slot = jnp.where(device < 0, device + ndev, device) * OWNED + (row & 3)
            cell = lax.broadcasted_iota(i32, (count, blocks), 1).astype(f32)
            found = jnp.where(position_row[...] == slot, cell, 0.0)
            named = jnp.sum(found, axis=1, keepdims=True).astype(i32)
            return jnp.broadcast_to(named, (count, 128))

        ids[...] = cells_of(ndev * 8, 3)
        ids_short[...] = cells_of(ndev * 4, 2)

        coarse = lax.broadcasted_iota(i32, (blocks, 128), 0)

        def look(i, seen):
            for n in range(8):
                seen = jnp.where(parent[pl.ds(i * 8 + n, 1), :] == coarse, 1.0, seen)
            return seen

        seen = lax.fori_loop(0, rows // 8, look, jnp.zeros((blocks, 128), f32))
        seen = jnp.broadcast_to(jnp.max(seen, axis=1, keepdims=True), (blocks, 128))
        below = (
            lax.broadcasted_iota(i32, (blocks, blocks), 1)
            < lax.broadcasted_iota(i32, (blocks, blocks), 0)
        )
        rank = jnp.dot(
            jnp.where(below, 1.0, 0.0).astype(bf16), seen.astype(bf16), preferred_element_type=f32
        )
        lanes = lax.broadcasted_iota(i32, (1, 128), 1)
        wanted = jnp.where(lanes < NAMED, lanes, jnp.where(lanes < 2 * NAMED, lanes - NAMED, -1))
        match = (rank == wanted.astype(f32)) & (seen > 0.0)
        list_row = jnp.sum(jnp.where(match, coarse.astype(f32) + 1.0, 0.0), axis=0, keepdims=True) - 1.0
        names_row[...] = jnp.broadcast_to(list_row, (8, 128)).astype(i32)
        names[...] = jnp.broadcast_to(list_row, (128, 128)).T[:NAMED].astype(i32)

        points = (lax.broadcasted_iota(i32, (ETA, 128), 0).astype(f32) + 0.5) / ETA
        log_a[...] = jnp.log(points)
        log_b[...] = jnp.log(1.0 - points)
        shape_sum = 1.0 / variance[...] - 1.0
        shape_a[...] = mean[...] * shape_sum - 1.0
        shape_b[...] = (1.0 - mean[...]) * shape_sum - 1.0

        for t in range(SPEC):
            columns[t] = jnp.broadcast_to(chem[:, t : t + 1], (SPEC, 128))

        spread = (
            (lax.broadcasted_iota(i32, (OWNED * SPEC, SPEC), 0) & (SPEC - 1))
            == lax.broadcasted_iota(i32, (OWNED * SPEC, SPEC), 1)
        ).astype(f32)
        weights = lax.dot_general(
            jnp.broadcast_to(weight[...], (OWNED, SPEC)), spread, NT,
            precision=HIGHEST, preferred_element_type=f32,
        )
        mine = lax.broadcasted_iota(i32, weights.shape, 0) == (
            lax.broadcasted_iota(i32, weights.shape, 1) >> 4
        )
        weights = jnp.where(mine, weights, 0.0)
        weights_of[...] = weights

    pending = []

    def hop(dz, dy, dx):
        def block(z, y, x):
            return state.at[
                core, lax.rem(x + xn, xn), lax.rem(z + zn, zn) * yn + lax.rem(y + yn, yn)
            ]

        if dy == 0 and dx == 0:
            there = (lax.rem(z + dz, zn) * yn + y, gy)
            here = block(z, y, x)
        else:
            there = (z * yn + lax.rem(y + dy, yn), lax.rem(x + dx, xn) * 2 + core)
            here = block(z - dz, y, x)
        come = block(z - dz, y - dy, x - dx)
        n = (dz * yn + dy) * xn + dx
        sems = (state_send.at[n], state_recv.at[n])
        return (
            pltpu.make_async_remote_copy(here, here, *sems, there, MESH),
            pltpu.make_async_remote_copy(come, come, *sems, there, MESH),
        )

    square = [(dy, dx) for dy in range(yn) for dx in range(xn) if dy or dx]

    def along_z(dz):
        return [hop(dz, 0, 0)]

    def over_square(dz):
        return [hop(dz, dy, dx) for dy, dx in square]

    def across(dz):
        there = (gx, x * 2 + 1 - core)
        part = pl.ds(lax.rem(z - dz + zn, zn) * yn, yn)
        here = state.at[core, :, part]
        come = state.at[1 - core, :, part]
        n = yn * xn * zn + dz
        sems = (state_send.at[n], state_recv.at[n])
        return [(
            pltpu.make_async_remote_copy(here, here, *sems, there, MESH),
            pltpu.make_async_remote_copy(come, come, *sems, there, MESH),
        )]

    def launch(copies):
        for out, _ in copies:
            out.start()
            pending.append(out)

    def arrive(copies):
        for _, come in copies:
            come.wait_recv()

    def halo(turn):
        low = (lax.rem(gx - 1 + gxn, gxn), gy)
        high = (lax.rem(gx + 1, gxn), gy)
        left = (gx, lax.rem(gy - 1 + gyn, gyn))
        right = (gx, lax.rem(gy + 1, gyn))
        source = grid if turn else thermal
        first = source.at[pl.ds(0, ys)]
        last = source.at[pl.ds((xs - 1) * ys, ys)]
        ends = [
            (last, face_x.at[turn, 0], high),
            (first, face_x.at[turn, 1], low),
            (own_y.at[turn], face_y.at[turn, 0], right),
            (own_y.at[turn], face_y.at[turn, 1], left),
        ]
        copies = [
            pltpu.make_async_remote_copy(
                s, d, halo_send.at[turn, n], halo_recv.at[turn, n], there, MESH
            )
            for n, (s, d, there) in enumerate(ends)
        ]
        return [(c, c) for c in copies]

    def send_halo(turn):
        now = grid[...]
        own_y[turn] = jnp.concatenate(
            [now[x * ys : x * ys + 1] for x in range(xs)]
            + [now[x * ys + ys - 1 : (x + 1) * ys] for x in range(xs)],
            axis=0,
        )
        launch(halo(turn))

    def exchange(source, target, turn, sign, send, recv):
        @pl.loop(1, ndev, unroll=unroll)
        def _(j):
            pltpu.make_async_remote_copy(
                source(j), target.at[turn, j], send.at[turn], recv.at[turn],
                place(me + sign * j), MESH,
            ).start()

        rest = target.at[turn, pl.ds(1, ndev - 1)]
        whole = pltpu.make_async_remote_copy(
            rest, rest, send.at[turn], recv.at[turn], place(me + 1), MESH
        )
        pending.append(whole)
        return whole

    half_row = lax.broadcasted_iota(i32, (8, 128), 0) < 4
    upper = (lax.broadcasted_iota(i32, (ndev * 8, 128), 0) & 4) == 0

    def split(values):
        high = values.astype(bf16)
        return [high, (values - high.astype(f32)).astype(bf16)]

    def hits(r):
        return parent[pl.ds(r, 1), :] == names[...]

    def gather_row(r, first):
        hit = hits(r)
        here = mass[pl.ds(r, 1), :]
        parts = [jnp.where(hit, here * chi[pl.ds(r, 1), :], 0.0).astype(bf16)]
        if first:
            parts = [jnp.where(hit, here, 0.0).astype(bf16)] + parts
        return jnp.concatenate(parts, axis=0)

    def add_up(chosen, values):
        chosen = jnp.concatenate(chosen, axis=1)
        count = chosen.shape[0]
        total[128 - 32 - count : 96] += lax.dot_general(
            chosen, values, NT, preferred_element_type=f32
        )

    def first_turn(i, cells):
        chosen = []
        for n in range(ROWS):
            r = i * ROWS + n
            logits = shape_a[pl.ds(r, 1), :] * log_a[...] + shape_b[pl.ds(r, 1), :] * log_b[...]
            raised = jnp.exp(logits - jnp.max(logits, axis=0, keepdims=True))
            part = raised * (1.0 / jnp.sum(raised, axis=0, keepdims=True))
            table[i, :, n * 128 : (n + 1) * 128] = part
            table16[i, :, n * 128 : (n + 1) * 128] = part.astype(bf16)
            chosen.append(gather_row(r, True))
        add_up(chosen, table16[i])
        each = blocks // turns
        for n in range(each):
            c = i * each + n
            at = position[c]
            cells = tuple(
                jnp.where(at == me * OWNED + q, c, cells[q]) for q in range(OWNED)
            )
        return cells

    def second_turn(i, carry):
        add_up([gather_row(i * ROWS + n, False) for n in range(ROWS)], table16[i])
        return carry

    def pick_sums(pick):
        pick = jnp.where(pick, 1.0, 0.0).astype(bf16)
        return jnp.dot(
            jnp.concatenate([pick, pick], axis=1),
            jnp.concatenate(split(total[...]), axis=0),
            preferred_element_type=f32,
        )

    def send_sums(turn):
        if turn == 0:
            low = lax.broadcasted_iota(i32, (ndev * 8, 128), 1) < NAMED
            sums = pick_sums((ids[...] == names_row[0:1, :]) & (low == upper))
            sent[0] = sums.reshape(ndev, 8, 128)
            return exchange(lambda j: sent.at[0, j], got, 0, -1, sums_send, sums_recv)
        low = lax.broadcasted_iota(i32, (ndev * 4, 128), 1) < NAMED
        sums = pick_sums((ids_short[...] == names_row[0:1, :]) & ~low)
        sent_short[0] = sums.reshape(ndev, 4, 128)
        return exchange(
            lambda j: sent_short.at[0, j], got_short, 0, -1, short_send, short_recv
        )

    def scalar_decay(turn):
        if turn == 0:
            sums = sent[0, 0] + jnp.sum(got[0, pl.ds(1, ndev - 1)], axis=0)
            weights_known[...] = sums[0:4]
            flux = sums[4:8]
        else:
            flux = sent_short[0, 0] + jnp.sum(got_short[0, pl.ds(1, ndev - 1)], axis=0)
        return (flux + prior_flux) / (weights_known[...] + prior_weight)

    def spread_rows(pieces):
        return jnp.concatenate(
            [jnp.broadcast_to(p, (SPEC, 128)) for p in pieces], axis=0
        )

    def block_of(slot):
        d = slot >> 2
        at = d & (gyn - 1)
        return state[at & 1, at >> 1, d >> (gyn.bit_length() - 1), pl.ds((slot & 3) * SPEC, SPEC), :]

    def laplacian(current):
        edge = lax.broadcasted_iota(i32, current.shape, 1)
        left = jnp.where(edge == 0, current, pltpu.roll(current, 1, 1))
        right = jnp.where(edge == 127, current, pltpu.roll(current, 127, 1))
        return right - 2.0 * current + left

    def advance(turn, cchi, cells):
        cchi = spread_rows([cchi[q : q + 1] for q in range(OWNED)])
        counts = jnp.concatenate(
            [jnp.full((SPEC, 128), increments[cells[q]] + 1, i32) for q in range(OWNED)], axis=0
        )
        fraction = 1.0 / counts.astype(f32)
        mixed = fraction * mixing_rate * cchi
        reacted = fraction * react_rate
        parts = []
        for q in range(OWNED):
            around = None
            for j in range(6):
                if turn == 0:
                    there = block_of(position[partners[j, cells[q]]])
                else:
                    n = (q * 6 + j) * SPEC
                    there = next_now[n : n + SPEC, :]
                around = there if around is None else around + there
            parts.append(around)
        around = jnp.concatenate(parts, axis=0)
        now = state0[...] if turn == 0 else result[: OWNED * SPEC]
        now = now + coupling * (around - 6.0 * now)

        def substep(index, current):
            bent_rows[...] = jnp.tanh(current)
            sources = [None] * OWNED
            for t in range(SPEC):
                column = columns[t]
                for q in range(OWNED):
                    term = column * bent_rows[q * SPEC + t : q * SPEC + t + 1, :]
                    sources[q] = term if t == 0 else sources[q] + term
            source = jnp.concatenate(sources, axis=0)
            update = mixed * laplacian(current) + reacted * source
            return jnp.where(index < counts, current + update, current)

        now = lax.fori_loop(0, SUBMAX, substep, now)
        result[: OWNED * SPEC] = now
        theta[turn, 0] = jnp.dot(weights_of[...], now, precision=HIGHEST, preferred_element_type=f32)

    def advance_near(cells):
        def prepare(j, carry):
            for q in range(OWNED):
                cell = partners[j, cells[q]]
                slot = position[cell]
                now = block_of(slot)
                around = None
                for k in range(6):
                    there = block_of(position[partners[k, cell]])
                    around = there if around is None else around + there
                d = me - (slot >> 2)
                d = jnp.where(d < 0, d + ndev, d)
                counts = jnp.full((SPEC, 128), increments[cell] + 1, i32)
                fraction = 1.0 / counts.astype(f32)
                rows_at = pl.ds((q * 6 + j) * SPEC, SPEC)
                next_now[rows_at, :] = now + coupling * (around - 6.0 * now)
                next_mixed[rows_at, :] = fraction * mixing_rate * known[0, d, pl.ds(slot & 3, 1), :]
                next_reacted[rows_at, :] = fraction * react_rate
                next_counts[rows_at, :] = counts
            return carry

        lax.fori_loop(0, 6, prepare, 0)

    def substeps_near(first, last):
        high, low = split(chem[...])
        chem_wide = jnp.concatenate([high, high, low], axis=1)

        def substep(index, carry):
            current = next_now[...]
            high, low = split(jnp.tanh(current))

            def side(values):
                return jnp.concatenate(
                    [values[n * SPEC : (n + 1) * SPEC] for n in range(6 * OWNED)], axis=1
                )

            high, low = side(high), side(low)
            source = jnp.dot(
                chem_wide, jnp.concatenate([high, low, high], axis=0), preferred_element_type=f32
            )
            source = jnp.concatenate(
                [source[:, n * 128 : (n + 1) * 128] for n in range(6 * OWNED)], axis=0
            )
            update = next_mixed[...] * laplacian(current) + next_reacted[...] * source
            next_now[...] = jnp.where(index < next_counts[...], current + update, current)
            return carry

        lax.fori_loop(first, last, substep, 0)

    def refine(turn):
        flat = theta[turn].reshape(ndev * 4, 128).T
        pick = jnp.where(ids_short[...] == names_row[0:1, :], 1.0, 0.0).astype(bf16)
        whole = jnp.dot(
            jnp.concatenate(split(flat), axis=1),
            jnp.concatenate([pick, pick], axis=0),
            preferred_element_type=f32,
        )
        high = whole.astype(bf16).astype(f32)
        lanes_all = lax.broadcasted_iota(i32, (ETA, 128), 1)
        halves = jnp.where(lanes_all < NAMED, high, whole - high).astype(bf16)
        blank = jnp.zeros((128 - 2 * NAMED, 128), bf16)

        def body(i, carry):
            picks = []
            for n in range(ROWS):
                hit = jnp.where(hits(i * ROWS + n), 1.0, 0.0).astype(bf16)
                picks.append(jnp.concatenate([hit, hit, blank], axis=0))
            picked = jnp.dot(
                halves, jnp.concatenate(picks, axis=1), preferred_element_type=f32
            )
            value = jnp.sum(table[i] * picked, axis=0, keepdims=True)
            for n in range(ROWS):
                fine[pl.ds(i * ROWS + n, 1), :] = value[:, n * 128 : (n + 1) * 128]
            return carry

        lax.fori_loop(0, turns, body, 0)

    def diffuse(turn):
        arrive(halo(turn))
        now = grid[...]
        zero = jnp.zeros((ys, 128), f32)
        low_x = jnp.where(gx == 0, zero, face_x[turn, 0])
        high_x = jnp.where(gx == gxn - 1, zero, face_x[turn, 1])
        around = jnp.concatenate([now[ys:], high_x], axis=0)
        around = around + jnp.concatenate([low_x, now[:-ys]], axis=0)
        low_y = jnp.where(gy == 0, 0.0, face_y[turn, 0])
        high_y = jnp.where(gy == gyn - 1, 0.0, face_y[turn, 1])
        low_y = jnp.concatenate(
            [jnp.broadcast_to(low_y[xs + x : xs + x + 1], (ys, 128)) for x in range(xs)], axis=0
        )
        high_y = jnp.concatenate(
            [jnp.broadcast_to(high_y[x : x + 1], (ys, 128)) for x in range(xs)], axis=0
        )
        y = lax.rem(lax.broadcasted_iota(i32, (rows, 128), 0), ys)
        around = around + jnp.where(y == ys - 1, high_y, pltpu.roll(now, rows - 1, 0))
        around = around + jnp.where(y == 0, low_y, pltpu.roll(now, 1, 0))
        z = lax.broadcasted_iota(i32, (rows, 128), 1)
        around = around + jnp.where(z == 127, 0.0, pltpu.roll(now, 127, 1))
        around = around + jnp.where(z == 0, 0.0, pltpu.roll(now, 1, 1))
        return (
            now
            + thermal_diffusion * (around - 6.0 * now)
            + damping_contribution * (fine[...] - now)
        )

    def dissipate():
        chi[...] = decay[...] * (1.0 + 0.5 * jnp.tanh(grid[...]))

    state[core, x, gx] = state0[...]
    for dz in range(1, zn):
        launch(along_z(dz))
    launch(over_square(0))
    loads[1].wait()
    grid[...] = thermal[...]
    send_halo(0)
    prepare_all()
    dissipate()
    total[...] = jnp.zeros_like(total)
    cells = (jnp.int32(0),) * OWNED
    cells = lax.fori_loop(0, turns // 2, first_turn, cells)
    for dz in range(1, zn):
        arrive(along_z(dz))
        launch(over_square(dz))
    cells = lax.fori_loop(turns // 2, turns, first_turn, cells)
    moving = send_sums(0)
    for dz in range(zn):
        arrive(over_square(dz))
        launch(across(dz))
    moving.wait_recv()
    cchi = scalar_decay(0)
    known[0, 0] = cchi
    all_known = exchange(lambda j: known.at[0, 0], known, 0, 1, known_send, known_recv)
    for dz in range(zn):
        arrive(across(dz))
    advance(0, cchi, cells)
    moving = exchange(lambda j: theta.at[0, 0], theta, 0, 1, theta_send, theta_recv)
    all_known.wait_recv()
    advance_near(cells)
    substeps_near(0, SUBMAX // 2)
    moving.wait_recv()
    refine(0)
    grid[...] = diffuse(0)

    send_halo(1)
    dissipate()
    total[...] = jnp.zeros_like(total)
    lax.fori_loop(0, turns, second_turn, 0)
    moving = send_sums(1)
    substeps_near(SUBMAX // 2, SUBMAX)
    moving.wait_recv()
    advance(1, scalar_decay(1), cells)
    exchange(lambda j: theta.at[1, 0], theta, 1, 1, theta_send, theta_recv).wait_recv()
    refine(1)
    result[OWNED * SPEC :] = diffuse(1)

    for copy in pending:
        copy.wait_send()


def shards(
    thermal_grid,
    average_blend_fraction,
    normalized_blend_variance,
    small_volume_mass,
    bare_scalar_decay,
    parent_block,
    species_given_block,
    block_position,
    face_partners,
    reaction_increments,
    chemical_coupling,
    species_thermal_weight,
):
    gxn, gyn = lax.axis_size("gx"), lax.axis_size("gy")
    ndev = gxn * gyn
    blocks = block_position.shape[0]
    xs, ys, zs = thermal_grid.shape
    rows = xs * ys
    turns = rows // ROWS
    assert ndev & (ndev - 1) == 0 and gyn & (gyn - 1) == 0
    assert blocks == ndev * OWNED and zs == 128 and rows % (2 * ROWS) == 0
    vmem = pl.BlockSpec(memory_space=pltpu.VMEM)
    dma = pltpu.SemaphoreType.DMA
    result = pl.pallas_call(
        functools.partial(kernel, gxn, gyn, xs, ys),
        out_shape=jax.ShapeDtypeStruct((OWNED * SPEC + rows, zs), f32),
        in_specs=[pl.BlockSpec(memory_space=pltpu.HBM)] * 13,
        out_specs=vmem,
        scratch_shapes=[
            *[pltpu.VMEM((rows, zs), f32)] * 5,
            pltpu.VMEM((rows, zs), i32),
            pltpu.VMEM((OWNED * SPEC, ETA), f32),
            pltpu.VMEM((1, blocks), i32),
            pltpu.VMEM((SPEC, SPEC), f32),
            pltpu.VMEM((1, SPEC), f32),
            pltpu.SMEM((blocks,), i32),
            pltpu.SMEM((6, blocks), i32),
            pltpu.SMEM((blocks,), i32),
            dma((13,)),
            pltpu.VMEM((ndev * 8, 128), i32),
            pltpu.VMEM((NAMED, 128), i32),
            pltpu.VMEM((8, 128), i32),
            pltpu.VMEM((OWNED * SPEC, ETA), f32),
            pltpu.VMEM((SPEC, SPEC, ETA), f32),
            pltpu.VMEM((4, ETA), f32),
            pltpu.VMEM((OWNED, OWNED * SPEC), f32),
            pltpu.VMEM((ndev * 4, 128), i32),
            pltpu.VMEM((ETA, 128), f32),
            pltpu.VMEM((ETA, 128), f32),
            pltpu.VMEM((rows, zs), f32),
            pltpu.VMEM((rows, zs), f32),
            pltpu.VMEM((rows, zs), f32),
            pltpu.VMEM((rows, zs), f32),
            pltpu.VMEM((rows, zs), f32),
            pltpu.VMEM((turns, ETA, ROWS * 128), f32),
            pltpu.VMEM((turns, ETA, ROWS * 128), bf16),
            pltpu.VMEM((128, ETA), f32),
            pltpu.VMEM((1, ndev, 4, ETA), f32),
            *[pltpu.VMEM((6 * OWNED * SPEC, ETA), f32)] * 3,
            pltpu.VMEM((6 * OWNED * SPEC, ETA), i32),
            pltpu.VMEM((1, ndev, 8, ETA), f32),
            pltpu.VMEM((1, ndev, 8, ETA), f32),
            pltpu.VMEM((1, ndev, 4, ETA), f32),
            pltpu.VMEM((1, ndev, 4, ETA), f32),
            pltpu.VMEM((STEPS, ndev, 4, ETA), f32),
            pltpu.VMEM((2, gyn // 2, gxn, OWNED * SPEC, ETA), f32),
            pltpu.VMEM((STEPS, 2, ys, zs), f32),
            pltpu.VMEM((STEPS, 2, 2 * xs, zs), f32),
            pltpu.VMEM((STEPS, 2 * xs, zs), f32),
            dma((1,)),
            dma((1,)),
            dma((1,)),
            dma((1,)),
            dma((1,)),
            dma((1,)),
            dma((STEPS,)),
            dma((STEPS,)),
            dma((ndev // 2 + gxn,)),
            dma((ndev // 2 + gxn,)),
            dma((STEPS, 4)),
            dma((STEPS, 4)),
        ],
        compiler_params=pltpu.CompilerParams(
            collective_id=0, has_side_effects=True, vmem_limit_bytes=63 * 1024 * 1024
        ),
    )(
        thermal_grid.reshape(rows, zs),
        average_blend_fraction.reshape(rows, zs),
        normalized_blend_variance.reshape(rows, zs),
        small_volume_mass.reshape(rows, zs),
        bare_scalar_decay.reshape(rows, zs),
        parent_block.reshape(rows, zs),
        species_given_block.reshape(OWNED * SPEC, ETA),
        block_position.reshape(1, blocks),
        chemical_coupling,
        species_thermal_weight.reshape(1, SPEC),
        block_position,
        face_partners.T,
        reaction_increments,
    )
    species, thermal = result[: OWNED * SPEC], result[OWNED * SPEC :]
    return (species.reshape(OWNED, SPEC, ETA), thermal.reshape(xs, ys, zs))


def solution(mesh):
    fine = P("gx", "gy", None)
    return jax.shard_map(
        shards,
        mesh=mesh,
        in_specs=(fine,) * 6 + (P(("gx", "gy"), None, None),) + (P(),) * 5,
        out_specs=(P(("gx", "gy"), None, None), fine),
        check_vma=False,
    )
```

```python
import functools

import jax
import jax.numpy as jnp
from jax import lax
from jax.experimental import pallas as pl
from jax.experimental.pallas import tpu as pltpu
from jax.sharding import PartitionSpec as P

ETA = 128
SPEC = 16
SUBMAX = 16
STEPS = 2
ROWS = 16
OWNED = 4
NAMED = 48

coupling = 0.05
mixing_rate = 0.2
react_rate = 0.5
prior_weight = 1.0
prior_flux = 0.5
thermal_diffusion = 0.1
damping_contribution = 0.3

MESH = pl.DeviceIdType.MESH
HIGHEST = lax.Precision.HIGHEST
NT = (((1,), (1,)), ((), ()))
f32, bf16, i32 = jnp.float32, jnp.bfloat16, jnp.int32


def kernel(
    gxn, gyn, xs, ys,
    thermal_in, mean_in, variance_in, mass_in, decay_in, parent_in, state0_in, position_row_in,
    chem_in, weight_in, position_in, partners_in, increments_in,
    result,
    thermal, mean, variance, mass, decay, parent, state0, position_row, chem, weight,
    position, partners, increments, load,
    ids, names, names_row, bent_rows, columns, weights_known, weights_of, ids_short, log_a, log_b, shape_a, shape_b, chi, grid, fine, table, table16, total,
    known, next_now, next_mixed, next_reacted, next_counts,
    sent, got, sent_short, got_short, theta, state, face_x, face_y, own_y,
    sums_send, sums_recv, short_send, short_recv, known_send, known_recv, theta_send, theta_recv, state_send, state_recv, halo_send, halo_recv,
):
    ndev = gxn * gyn
    blocks = ndev * OWNED
    rows = xs * ys
    turns = rows // ROWS
    unroll = ndev - 1 if ndev <= 32 else 1
    xn = gyn // 2
    yn = xn if gxn % xn == 0 else 1
    zn = gxn // yn
    gx, gy = lax.axis_index("gx"), lax.axis_index("gy")
    me = gx * gyn + gy
    core, x = gy & 1, gy >> 1
    y, z = lax.rem(gx, yn), gx // yn

    def place(device):
        device = (device + ndev) & (ndev - 1)
        return (device >> (gyn.bit_length() - 1), device & (gyn - 1))

    barrier = pltpu.get_barrier_semaphore()

    @pl.loop(1, ndev, unroll=unroll)
    def _(j):
        pl.semaphore_signal(barrier, inc=1, device_id=place(me + j), device_id_type=MESH)

    loads = [
        pltpu.make_async_copy(source, target, load.at[n])
        for n, (source, target) in enumerate((
            (state0_in, state0), (thermal_in, thermal), (position_row_in, position_row),
            (parent_in, parent), (variance_in, variance), (mean_in, mean), (mass_in, mass),
            (decay_in, decay), (chem_in, chem), (weight_in, weight),
            (position_in, position), (partners_in, partners), (increments_in, increments),
        ))
    ]
    for copy in loads:
        copy.start()
    loads[0].wait()
    pl.semaphore_wait(barrier, ndev - 1)

    def prepare_all():
        for copy in loads[2:]:
            copy.wait()
        def cells_of(count, shift):
            row = lax.broadcasted_iota(i32, (count, blocks), 0)
            device = me - (row >> shift)
            slot = jnp.where(device < 0, device + ndev, device) * OWNED + (row & 3)
            cell = lax.broadcasted_iota(i32, (count, blocks), 1).astype(f32)
            found = jnp.where(position_row[...] == slot, cell, 0.0)
            named = jnp.sum(found, axis=1, keepdims=True).astype(i32)
            return jnp.broadcast_to(named, (count, 128))

        ids[...] = cells_of(ndev * 8, 3)
        ids_short[...] = cells_of(ndev * 4, 2)

        coarse = lax.broadcasted_iota(i32, (blocks, 128), 0)

        def look(i, seen):
            for n in range(8):
                seen = jnp.where(parent[pl.ds(i * 8 + n, 1), :] == coarse, 1.0, seen)
            return seen

        seen = lax.fori_loop(0, rows // 8, look, jnp.zeros((blocks, 128), f32))
        seen = jnp.broadcast_to(jnp.max(seen, axis=1, keepdims=True), (blocks, 128))
        below = (
            lax.broadcasted_iota(i32, (blocks, blocks), 1)
            < lax.broadcasted_iota(i32, (blocks, blocks), 0)
        )
        rank = jnp.dot(
            jnp.where(below, 1.0, 0.0).astype(bf16), seen.astype(bf16), preferred_element_type=f32
        )
        lanes = lax.broadcasted_iota(i32, (1, 128), 1)
        wanted = jnp.where(lanes < NAMED, lanes, jnp.where(lanes < 2 * NAMED, lanes - NAMED, -1))
        match = (rank == wanted.astype(f32)) & (seen > 0.0)
        list_row = jnp.sum(jnp.where(match, coarse.astype(f32) + 1.0, 0.0), axis=0, keepdims=True) - 1.0
        names_row[...] = jnp.broadcast_to(list_row, (8, 128)).astype(i32)
        names[...] = jnp.broadcast_to(list_row, (128, 128)).T[:NAMED].astype(i32)

        points = (lax.broadcasted_iota(i32, (ETA, 128), 0).astype(f32) + 0.5) / ETA
        log_a[...] = jnp.log(points)
        log_b[...] = jnp.log(1.0 - points)
        shape_sum = 1.0 / variance[...] - 1.0
        shape_a[...] = mean[...] * shape_sum - 1.0
        shape_b[...] = (1.0 - mean[...]) * shape_sum - 1.0

        for t in range(SPEC):
            columns[t] = jnp.broadcast_to(chem[:, t : t + 1], (SPEC, 128))

        spread = (
            (lax.broadcasted_iota(i32, (OWNED * SPEC, SPEC), 0) & (SPEC - 1))
            == lax.broadcasted_iota(i32, (OWNED * SPEC, SPEC), 1)
        ).astype(f32)
        weights = lax.dot_general(
            jnp.broadcast_to(weight[...], (OWNED, SPEC)), spread, NT,
            precision=HIGHEST, preferred_element_type=f32,
        )
        mine = lax.broadcasted_iota(i32, weights.shape, 0) == (
            lax.broadcasted_iota(i32, weights.shape, 1) >> 4
        )
        weights = jnp.where(mine, weights, 0.0)
        weights_of[...] = weights

    pending = []

    def hop(dz, dy, dx):
        def block(z, y, x):
            return state.at[
                core, lax.rem(x + xn, xn), lax.rem(z + zn, zn) * yn + lax.rem(y + yn, yn)
            ]

        if dy == 0 and dx == 0:
            there = (lax.rem(z + dz, zn) * yn + y, gy)
            here = block(z, y, x)
        else:
            there = (z * yn + lax.rem(y + dy, yn), lax.rem(x + dx, xn) * 2 + core)
            here = block(z - dz, y, x)
        come = block(z - dz, y - dy, x - dx)
        n = (dz * yn + dy) * xn + dx
        sems = (state_send.at[n], state_recv.at[n])
        return (
            pltpu.make_async_remote_copy(here, here, *sems, there, MESH),
            pltpu.make_async_remote_copy(come, come, *sems, there, MESH),
        )

    square = [(dy, dx) for dy in range(yn) for dx in range(xn) if dy or dx]

    def along_z(dz):
        return [hop(dz, 0, 0)]

    def over_square(dz):
        return [hop(dz, dy, dx) for dy, dx in square]

    def across(dz):
        there = (gx, x * 2 + 1 - core)
        part = pl.ds(lax.rem(z - dz + zn, zn) * yn, yn)
        here = state.at[core, :, part]
        come = state.at[1 - core, :, part]
        n = yn * xn * zn + dz
        sems = (state_send.at[n], state_recv.at[n])
        return [(
            pltpu.make_async_remote_copy(here, here, *sems, there, MESH),
            pltpu.make_async_remote_copy(come, come, *sems, there, MESH),
        )]

    def launch(copies):
        for out, _ in copies:
            out.start()
            pending.append(out)

    def arrive(copies):
        for _, come in copies:
            come.wait_recv()

    def halo(turn):
        low = (lax.rem(gx - 1 + gxn, gxn), gy)
        high = (lax.rem(gx + 1, gxn), gy)
        left = (gx, lax.rem(gy - 1 + gyn, gyn))
        right = (gx, lax.rem(gy + 1, gyn))
        source = grid if turn else thermal
        first = source.at[pl.ds(0, ys)]
        last = source.at[pl.ds((xs - 1) * ys, ys)]
        ends = [
            (last, face_x.at[turn, 0], high),
            (first, face_x.at[turn, 1], low),
            (own_y.at[turn], face_y.at[turn, 0], right),
            (own_y.at[turn], face_y.at[turn, 1], left),
        ]
        copies = [
            pltpu.make_async_remote_copy(
                s, d, halo_send.at[turn, n], halo_recv.at[turn, n], there, MESH
            )
            for n, (s, d, there) in enumerate(ends)
        ]
        return [(c, c) for c in copies]

    def send_halo(turn):
        now = grid[...]
        own_y[turn] = jnp.concatenate(
            [now[x * ys : x * ys + 1] for x in range(xs)]
            + [now[x * ys + ys - 1 : (x + 1) * ys] for x in range(xs)],
            axis=0,
        )
        launch(halo(turn))

    def exchange(source, target, turn, sign, send, recv):
        @pl.loop(1, ndev, unroll=unroll)
        def _(j):
            pltpu.make_async_remote_copy(
                source(j), target.at[turn, j], send.at[turn], recv.at[turn],
                place(me + sign * j), MESH,
            ).start()

        rest = target.at[turn, pl.ds(1, ndev - 1)]
        whole = pltpu.make_async_remote_copy(
            rest, rest, send.at[turn], recv.at[turn], place(me + 1), MESH
        )
        pending.append(whole)
        return whole

    half_row = lax.broadcasted_iota(i32, (8, 128), 0) < 4
    upper = (lax.broadcasted_iota(i32, (ndev * 8, 128), 0) & 4) == 0

    def split(values):
        high = values.astype(bf16)
        return [high, (values - high.astype(f32)).astype(bf16)]

    def hits(r):
        return parent[pl.ds(r, 1), :] == names[...]

    def gather_row(r, first):
        hit = hits(r)
        here = mass[pl.ds(r, 1), :]
        parts = [jnp.where(hit, here * chi[pl.ds(r, 1), :], 0.0).astype(bf16)]
        if first:
            parts = [jnp.where(hit, here, 0.0).astype(bf16)] + parts
        return jnp.concatenate(parts, axis=0)

    def add_up(chosen, values):
        chosen = jnp.concatenate(chosen, axis=1)
        count = chosen.shape[0]
        total[128 - 32 - count : 96] += lax.dot_general(
            chosen, values, NT, preferred_element_type=f32
        )

    def first_turn(i, cells):
        chosen = []
        for n in range(ROWS):
            r = i * ROWS + n
            logits = shape_a[pl.ds(r, 1), :] * log_a[...] + shape_b[pl.ds(r, 1), :] * log_b[...]
            raised = jnp.exp(logits - jnp.max(logits, axis=0, keepdims=True))
            part = raised * (1.0 / jnp.sum(raised, axis=0, keepdims=True))
            table[i, :, n * 128 : (n + 1) * 128] = part
            table16[i, :, n * 128 : (n + 1) * 128] = part.astype(bf16)
            chosen.append(gather_row(r, True))
        add_up(chosen, table16[i])
        each = blocks // turns
        for n in range(each):
            c = i * each + n
            at = position[c]
            cells = tuple(
                jnp.where(at == me * OWNED + q, c, cells[q]) for q in range(OWNED)
            )
        return cells

    def second_turn(i, carry):
        add_up([gather_row(i * ROWS + n, False) for n in range(ROWS)], table16[i])
        return carry

    def pick_sums(pick):
        pick = jnp.where(pick, 1.0, 0.0).astype(bf16)
        return jnp.dot(
            jnp.concatenate([pick, pick], axis=1),
            jnp.concatenate(split(total[...]), axis=0),
            preferred_element_type=f32,
        )

    def send_sums(turn):
        if turn == 0:
            low = lax.broadcasted_iota(i32, (ndev * 8, 128), 1) < NAMED
            sums = pick_sums((ids[...] == names_row[0:1, :]) & (low == upper))
            sent[0] = sums.reshape(ndev, 8, 128)
            return exchange(lambda j: sent.at[0, j], got, 0, -1, sums_send, sums_recv)
        low = lax.broadcasted_iota(i32, (ndev * 4, 128), 1) < NAMED
        sums = pick_sums((ids_short[...] == names_row[0:1, :]) & ~low)
        sent_short[0] = sums.reshape(ndev, 4, 128)
        return exchange(
            lambda j: sent_short.at[0, j], got_short, 0, -1, short_send, short_recv
        )

    def scalar_decay(turn):
        if turn == 0:
            sums = sent[0, 0] + jnp.sum(got[0, pl.ds(1, ndev - 1)], axis=0)
            weights_known[...] = sums[0:4]
            flux = sums[4:8]
        else:
            flux = sent_short[0, 0] + jnp.sum(got_short[0, pl.ds(1, ndev - 1)], axis=0)
        return (flux + prior_flux) / (weights_known[...] + prior_weight)

    def spread_rows(pieces):
        return jnp.concatenate(
            [jnp.broadcast_to(p, (SPEC, 128)) for p in pieces], axis=0
        )

    def block_of(slot):
        d = slot >> 2
        at = d & (gyn - 1)
        return state[at & 1, at >> 1, d >> (gyn.bit_length() - 1), pl.ds((slot & 3) * SPEC, SPEC), :]

    def laplacian(current):
        edge = lax.broadcasted_iota(i32, current.shape, 1)
        left = jnp.where(edge == 0, current, pltpu.roll(current, 1, 1))
        right = jnp.where(edge == 127, current, pltpu.roll(current, 127, 1))
        return right - 2.0 * current + left

    def advance(turn, cchi, cells):
        cchi = spread_rows([cchi[q : q + 1] for q in range(OWNED)])
        counts = jnp.concatenate(
            [jnp.full((SPEC, 128), increments[cells[q]] + 1, i32) for q in range(OWNED)], axis=0
        )
        fraction = 1.0 / counts.astype(f32)
        mixed = fraction * mixing_rate * cchi
        reacted = fraction * react_rate
        parts = []
        for q in range(OWNED):
            around = None
            for j in range(6):
                if turn == 0:
                    there = block_of(position[partners[j, cells[q]]])
                else:
                    n = (q * 6 + j) * SPEC
                    there = next_now[n : n + SPEC, :]
                around = there if around is None else around + there
            parts.append(around)
        around = jnp.concatenate(parts, axis=0)
        now = state0[...] if turn == 0 else result[: OWNED * SPEC]
        now = now + coupling * (around - 6.0 * now)

        def substep(index, current):
            bent_rows[...] = jnp.tanh(current)
            sources = [None] * (2 * OWNED)
            for t in range(SPEC):
                column = columns[t]
                for q in range(OWNED):
                    term = column * bent_rows[q * SPEC + t : q * SPEC + t + 1, :]
                    n = q * 2 + (t & 1)
                    sources[n] = term if t < 2 else sources[n] + term
            source = jnp.concatenate(
                [sources[2 * q] + sources[2 * q + 1] for q in range(OWNED)], axis=0
            )
            update = mixed * laplacian(current) + reacted * source
            return jnp.where(index < counts, current + update, current)

        now = lax.fori_loop(0, SUBMAX, substep, now)
        result[: OWNED * SPEC] = now
        theta[turn, 0] = jnp.dot(weights_of[...], now, precision=HIGHEST, preferred_element_type=f32)

    def advance_near(cells):
        def prepare(j, carry):
            for q in range(OWNED):
                cell = partners[j, cells[q]]
                slot = position[cell]
                now = block_of(slot)
                around = None
                for k in range(6):
                    there = block_of(position[partners[k, cell]])
                    around = there if around is None else around + there
                d = me - (slot >> 2)
                d = jnp.where(d < 0, d + ndev, d)
                counts = jnp.full((SPEC, 128), increments[cell] + 1, i32)
                fraction = 1.0 / counts.astype(f32)
                rows_at = pl.ds((q * 6 + j) * SPEC, SPEC)
                next_now[rows_at, :] = now + coupling * (around - 6.0 * now)
                next_mixed[rows_at, :] = fraction * mixing_rate * known[0, d, pl.ds(slot & 3, 1), :]
                next_reacted[rows_at, :] = fraction * react_rate
                next_counts[rows_at, :] = counts
            return carry

        lax.fori_loop(0, 6, prepare, 0)

    def substeps_near(first, last):
        high, low = split(chem[...])
        chem_wide = jnp.concatenate([high, high, low], axis=1)

        def substep(index, carry):
            current = next_now[...]
            high, low = split(jnp.tanh(current))

            def side(values):
                return jnp.concatenate(
                    [values[n * SPEC : (n + 1) * SPEC] for n in range(6 * OWNED)], axis=1
                )

            high, low = side(high), side(low)
            source = jnp.dot(
                chem_wide, jnp.concatenate([high, low, high], axis=0), preferred_element_type=f32
            )
            source = jnp.concatenate(
                [source[:, n * 128 : (n + 1) * 128] for n in range(6 * OWNED)], axis=0
            )
            update = next_mixed[...] * laplacian(current) + next_reacted[...] * source
            next_now[...] = jnp.where(index < next_counts[...], current + update, current)
            return carry

        lax.fori_loop(first, last, substep, 0)

    def refine(turn):
        flat = theta[turn].reshape(ndev * 4, 128).T
        pick = jnp.where(ids_short[...] == names_row[0:1, :], 1.0, 0.0).astype(bf16)
        whole = jnp.dot(
            jnp.concatenate(split(flat), axis=1),
            jnp.concatenate([pick, pick], axis=0),
            preferred_element_type=f32,
        )
        high = whole.astype(bf16).astype(f32)
        lanes_all = lax.broadcasted_iota(i32, (ETA, 128), 1)
        halves = jnp.where(lanes_all < NAMED, high, whole - high).astype(bf16)
        blank = jnp.zeros((128 - 2 * NAMED, 128), bf16)

        def body(i, carry):
            picks = []
            for n in range(ROWS):
                hit = jnp.where(hits(i * ROWS + n), 1.0, 0.0).astype(bf16)
                picks.append(jnp.concatenate([hit, hit, blank], axis=0))
            picked = jnp.dot(
                halves, jnp.concatenate(picks, axis=1), preferred_element_type=f32
            )
            value = jnp.sum(table[i] * picked, axis=0, keepdims=True)
            for n in range(ROWS):
                fine[pl.ds(i * ROWS + n, 1), :] = value[:, n * 128 : (n + 1) * 128]
            return carry

        lax.fori_loop(0, turns, body, 0)

    def diffuse(turn):
        arrive(halo(turn))
        now = grid[...]
        zero = jnp.zeros((ys, 128), f32)
        low_x = jnp.where(gx == 0, zero, face_x[turn, 0])
        high_x = jnp.where(gx == gxn - 1, zero, face_x[turn, 1])
        around = jnp.concatenate([now[ys:], high_x], axis=0)
        around = around + jnp.concatenate([low_x, now[:-ys]], axis=0)
        low_y = jnp.where(gy == 0, 0.0, face_y[turn, 0])
        high_y = jnp.where(gy == gyn - 1, 0.0, face_y[turn, 1])
        low_y = jnp.concatenate(
            [jnp.broadcast_to(low_y[xs + x : xs + x + 1], (ys, 128)) for x in range(xs)], axis=0
        )
        high_y = jnp.concatenate(
            [jnp.broadcast_to(high_y[x : x + 1], (ys, 128)) for x in range(xs)], axis=0
        )
        y = lax.rem(lax.broadcasted_iota(i32, (rows, 128), 0), ys)
        around = around + jnp.where(y == ys - 1, high_y, pltpu.roll(now, rows - 1, 0))
        around = around + jnp.where(y == 0, low_y, pltpu.roll(now, 1, 0))
        z = lax.broadcasted_iota(i32, (rows, 128), 1)
        around = around + jnp.where(z == 127, 0.0, pltpu.roll(now, 127, 1))
        around = around + jnp.where(z == 0, 0.0, pltpu.roll(now, 1, 1))
        return (
            now
            + thermal_diffusion * (around - 6.0 * now)
            + damping_contribution * (fine[...] - now)
        )

    def dissipate():
        chi[...] = decay[...] * (1.0 + 0.5 * jnp.tanh(grid[...]))

    state[core, x, gx] = state0[...]
    for dz in range(1, zn):
        launch(along_z(dz))
    launch(over_square(0))
    loads[1].wait()
    grid[...] = thermal[...]
    send_halo(0)
    prepare_all()
    dissipate()
    total[...] = jnp.zeros_like(total)
    cells = (jnp.int32(0),) * OWNED
    cells = lax.fori_loop(0, turns // 2, first_turn, cells)
    for dz in range(1, zn):
        arrive(along_z(dz))
        launch(over_square(dz))
    cells = lax.fori_loop(turns // 2, turns, first_turn, cells)
    moving = send_sums(0)
    for dz in range(zn):
        arrive(over_square(dz))
        launch(across(dz))
    moving.wait_recv()
    cchi = scalar_decay(0)
    known[0, 0] = cchi
    all_known = exchange(lambda j: known.at[0, 0], known, 0, 1, known_send, known_recv)
    for dz in range(zn):
        arrive(across(dz))
    advance(0, cchi, cells)
    moving = exchange(lambda j: theta.at[0, 0], theta, 0, 1, theta_send, theta_recv)
    all_known.wait_recv()
    advance_near(cells)
    substeps_near(0, SUBMAX // 2)
    moving.wait_recv()
    refine(0)
    grid[...] = diffuse(0)

    send_halo(1)
    dissipate()
    total[...] = jnp.zeros_like(total)
    lax.fori_loop(0, turns, second_turn, 0)
    moving = send_sums(1)
    substeps_near(SUBMAX // 2, SUBMAX)
    moving.wait_recv()
    advance(1, scalar_decay(1), cells)
    exchange(lambda j: theta.at[1, 0], theta, 1, 1, theta_send, theta_recv).wait_recv()
    refine(1)
    result[OWNED * SPEC :] = diffuse(1)

    for copy in pending:
        copy.wait_send()


def shards(
    thermal_grid,
    average_blend_fraction,
    normalized_blend_variance,
    small_volume_mass,
    bare_scalar_decay,
    parent_block,
    species_given_block,
    block_position,
    face_partners,
    reaction_increments,
    chemical_coupling,
    species_thermal_weight,
):
    gxn, gyn = lax.axis_size("gx"), lax.axis_size("gy")
    ndev = gxn * gyn
    blocks = block_position.shape[0]
    xs, ys, zs = thermal_grid.shape
    rows = xs * ys
    turns = rows // ROWS
    assert ndev & (ndev - 1) == 0 and gyn & (gyn - 1) == 0
    assert blocks == ndev * OWNED and zs == 128 and rows % (2 * ROWS) == 0
    vmem = pl.BlockSpec(memory_space=pltpu.VMEM)
    dma = pltpu.SemaphoreType.DMA
    result = pl.pallas_call(
        functools.partial(kernel, gxn, gyn, xs, ys),
        out_shape=jax.ShapeDtypeStruct((OWNED * SPEC + rows, zs), f32),
        in_specs=[pl.BlockSpec(memory_space=pltpu.HBM)] * 13,
        out_specs=vmem,
        scratch_shapes=[
            *[pltpu.VMEM((rows, zs), f32)] * 5,
            pltpu.VMEM((rows, zs), i32),
            pltpu.VMEM((OWNED * SPEC, ETA), f32),
            pltpu.VMEM((1, blocks), i32),
            pltpu.VMEM((SPEC, SPEC), f32),
            pltpu.VMEM((1, SPEC), f32),
            pltpu.SMEM((blocks,), i32),
            pltpu.SMEM((6, blocks), i32),
            pltpu.SMEM((blocks,), i32),
            dma((13,)),
            pltpu.VMEM((ndev * 8, 128), i32),
            pltpu.VMEM((NAMED, 128), i32),
            pltpu.VMEM((8, 128), i32),
            pltpu.VMEM((OWNED * SPEC, ETA), f32),
            pltpu.VMEM((SPEC, SPEC, ETA), f32),
            pltpu.VMEM((4, ETA), f32),
            pltpu.VMEM((OWNED, OWNED * SPEC), f32),
            pltpu.VMEM((ndev * 4, 128), i32),
            pltpu.VMEM((ETA, 128), f32),
            pltpu.VMEM((ETA, 128), f32),
            pltpu.VMEM((rows, zs), f32),
            pltpu.VMEM((rows, zs), f32),
            pltpu.VMEM((rows, zs), f32),
            pltpu.VMEM((rows, zs), f32),
            pltpu.VMEM((rows, zs), f32),
            pltpu.VMEM((turns, ETA, ROWS * 128), f32),
            pltpu.VMEM((turns, ETA, ROWS * 128), bf16),
            pltpu.VMEM((128, ETA), f32),
            pltpu.VMEM((1, ndev, 4, ETA), f32),
            *[pltpu.VMEM((6 * OWNED * SPEC, ETA), f32)] * 3,
            pltpu.VMEM((6 * OWNED * SPEC, ETA), i32),
            pltpu.VMEM((1, ndev, 8, ETA), f32),
            pltpu.VMEM((1, ndev, 8, ETA), f32),
            pltpu.VMEM((1, ndev, 4, ETA), f32),
            pltpu.VMEM((1, ndev, 4, ETA), f32),
            pltpu.VMEM((STEPS, ndev, 4, ETA), f32),
            pltpu.VMEM((2, gyn // 2, gxn, OWNED * SPEC, ETA), f32),
            pltpu.VMEM((STEPS, 2, ys, zs), f32),
            pltpu.VMEM((STEPS, 2, 2 * xs, zs), f32),
            pltpu.VMEM((STEPS, 2 * xs, zs), f32),
            dma((1,)),
            dma((1,)),
            dma((1,)),
            dma((1,)),
            dma((1,)),
            dma((1,)),
            dma((STEPS,)),
            dma((STEPS,)),
            dma((ndev // 2 + gxn,)),
            dma((ndev // 2 + gxn,)),
            dma((STEPS, 4)),
            dma((STEPS, 4)),
        ],
        compiler_params=pltpu.CompilerParams(
            collective_id=0, has_side_effects=True, vmem_limit_bytes=63 * 1024 * 1024
        ),
    )(
        thermal_grid.reshape(rows, zs),
        average_blend_fraction.reshape(rows, zs),
        normalized_blend_variance.reshape(rows, zs),
        small_volume_mass.reshape(rows, zs),
        bare_scalar_decay.reshape(rows, zs),
        parent_block.reshape(rows, zs),
        species_given_block.reshape(OWNED * SPEC, ETA),
        block_position.reshape(1, blocks),
        chemical_coupling,
        species_thermal_weight.reshape(1, SPEC),
        block_position,
        face_partners.T,
        reaction_increments,
    )
    species, thermal = result[: OWNED * SPEC], result[OWNED * SPEC :]
    return (species.reshape(OWNED, SPEC, ETA), thermal.reshape(xs, ys, zs))


def solution(mesh):
    fine = P("gx", "gy", None)
    return jax.shard_map(
        shards,
        mesh=mesh,
        in_specs=(fine,) * 6 + (P(("gx", "gy"), None, None),) + (P(),) * 5,
        out_specs=(P(("gx", "gy"), None, None), fine),
        check_vma=False,
    )
```
